256 devices in a mesh: tm: 64 (over z, y, core), rec: 4 (over x).
Axes of the slice: x: 4, y: 4, z: 8, core: 2. Of those that a mesh axis runs over, the one named last changes fastest.
Arguments:
- activations: bfloat16 [8, 16384, 512], P('rec', 'tm'), may hold values from -16 to 16
- cotangent: bfloat16 [8, 16384, 512], P('rec', 'tm'), may hold values from -6 to 6
- retain: float32 [8, 16384], P('rec', 'tm'), may hold values from 0.5 to 1
- dilation: int32 [9], replicated, may hold values from 0 to 128, as said below
- conv_w: float32 [9, 512], replicated, may hold values from -2 to 2
- skip_gain: float32 [512], replicated, may hold values from -6 to 6
- log_rate: float32 [512], replicated
- mode_angle: float32 [512], replicated, may hold values from -3.140625 to 3.140625
- w_in: bfloat16 [512, 1024], replicated, may hold values from -0.25 to 0.25
- w_out: bfloat16 [1024, 512], replicated, may hold values from -0.1875 to 0.1875
Outputs:
- grad_input: bfloat16 [8, 16384, 512], P('rec', 'tm')
- grad_taps: float32 [9, 512], replicated
- grad_skip: float32 [512], replicated
- grad_log_rate: float32 [512], replicated
- grad_angle: float32 [512], replicated
- grad_w_in: float32 [512, 1024], P('tm')
- grad_w_out: float32 [1024, 512], P('tm')
The draws below stay inside these ranges and needn't reach their ends.
Inputs may be any that keep to these rules, and one draw needn't show every extreme that they name: dilation[0] is 0, dilation[8] is 128, and the lags rise strictly.
All inputs are finite; a program needn't handle non-finite values.
Results may differ from the reference program's by a relative error of at most 0.01235.
Values may be sent and summed in bfloat16 or wider, within the bound.
A program may use at most 64 MiB of HBM per device.

```python
import math
from functools import partial
import jax
import jax.numpy as jnp
from jax import lax

D = 512
MODES = 512
TAPS = 9
MAXLAG = 128
RECORDS = 8
LEN = 16384


def draw_log_rate(key, part):
    key = jax.random.fold_in(key, 11)
    pick_key, slow_key, fast_key = jax.random.split(key, 3)
    slow_share = 0.5
    chosen = jax.random.uniform(pick_key, (MODES,)) < slow_share
    low_slow = jnp.log(0.02 / LEN)
    high_slow = jnp.log(0.5 / LEN)
    slow_value = low_slow + (high_slow - low_slow) * jax.random.uniform(slow_key, (MODES,))
    low_fast = jnp.log(1.0 / 60.0)
    high_fast = jnp.log(1.0 / 20.0)
    fast_value = low_fast + (high_fast - low_fast) * jax.random.uniform(fast_key, (MODES,))
    return jnp.where(chosen, slow_value, fast_value).astype(jnp.float32)


def draw_retain(key, part):
    key = jax.random.fold_in(key, 23)
    base_key, first_key, second_key, depth_key = jax.random.split(key, 4)
    base_keep = jnp.exp(-jax.random.uniform(base_key, (RECORDS, LEN)) * (0.3 / LEN))
    first_spot = jax.random.randint(first_key, (RECORDS,), 0, LEN)
    second_spot = (first_spot + 1 + jax.random.randint(second_key, (RECORDS,), 0, LEN - 1)) % LEN
    spots = jnp.stack([first_spot, second_spot], axis=1)
    depth = jax.random.uniform(depth_key, (RECORDS, 2), minval=0.55, maxval=0.8)
    places = jnp.arange(LEN)[None, :, None] == spots[:, None, :]
    factor = jnp.prod(jnp.where(places, depth[:, None, :], 1.0), axis=2)
    return (base_keep * factor).astype(jnp.float32)


def draw_dilation(key, part):
    key = jax.random.fold_in(key, 37)
    shuffled = jax.random.permutation(key, MAXLAG - 1)[:TAPS - 2] + 1
    middle = jnp.sort(shuffled).astype(jnp.int32)
    first_lag = jnp.zeros((1,), jnp.int32)
    last_lag = jnp.full((1,), MAXLAG, jnp.int32)
    return jnp.concatenate([first_lag, middle, last_lag])


def spiked(array, key, source, target, blocks, factor):
    owner, partner = [(jnp.arange(array.shape[position]) // (array.shape[position] // blocks)).reshape([-1 if axis == position else 1 for axis in range(array.ndim)]) for position in (source, target)]
    chosen = jax.random.permutation(key, blocks)[partner]
    strong = (owner == chosen) | (owner == (partner + blocks // 2) % blocks)
    return jnp.where(strong, factor * array, array)


def steps_of(own_key, shape, pieces, least, largest):
    def one(dim, parts):
        draws = jax.random.uniform(jax.random.fold_in(jax.random.fold_in(own_key, 6), dim), (parts,), jnp.float32, least / len(pieces), largest / len(pieces))
        return jnp.repeat(jnp.exp(draws), shape[dim] // parts).reshape((-1,) + (1,) * (len(shape) - dim - 1))

    gain = one(*pieces[0])
    for cut in pieces[1:]:
        gain = gain * one(*cut)
    return gain


def gaussian(own_key, extent, deviation, reach, shards=(), held_as=jnp.bfloat16):
    loudness = steps_of(own_key, extent, shards, -0.22, 0.18) if shards else 1.0
    entries = jax.random.normal(own_key, extent, jnp.float32) * deviation * loudness
    return jnp.minimum(jnp.maximum(entries, -reach), reach).astype(held_as)


def noise_with(rng, extent, width, bound, cuts, heavy, kind=jnp.bfloat16):
    result = width * jax.random.normal(rng, extent, jnp.float32)
    if cuts:
        result = result * steps_of(rng, extent, cuts, -0.22, 0.18)
    return jnp.clip(spiked(result, jax.random.fold_in(rng, 3), *heavy), -bound, bound).astype(kind)


def setup_inputs(seed: int = 0) -> dict:
    splits = jax.random.split(jax.random.key(seed), 11)
    activations = noise_with(splits[0], (RECORDS, LEN, D), 1.0, 16.0, ((0, 4), (1, 64)), (1, 2, 64, 4.0))
    cotangent = gaussian(splits[1], (RECORDS, LEN, D), 1.0, 6.0, ((0, 4), (1, 64)))
    retain = draw_retain(jax.random.fold_in(splits[10], 71), 0)
    dilation = draw_dilation(jax.random.fold_in(splits[10], 71), 0)
    conv_w = gaussian(splits[4], (TAPS, D), 0.33, 2.0, (), jnp.float32)
    skip_gain = gaussian(splits[5], (D,), 1.0, 6.0, (), jnp.float32)
    log_rate = draw_log_rate(jax.random.fold_in(splits[10], 71), 0)
    mode_angle = jnp.clip(jax.random.uniform(splits[7], (MODES,), jnp.float32, -3.140625, 3.140625), -3.140625, 3.140625)
    w_in = gaussian(splits[8], (D, 2 * MODES), D ** -0.5, 0.25)
    w_out = gaussian(splits[9], (2 * MODES, D), (2 * MODES) ** -0.5, 0.1875)
    return dict(activations=activations, cotangent=cotangent, retain=retain, dilation=dilation, conv_w=conv_w, skip_gain=skip_gain, log_rate=log_rate, mode_angle=mode_angle, w_in=w_in, w_out=w_out)


def decay_params(log_rate, mode_angle):
    decay_rate = jnp.exp(log_rate)
    radius = jnp.exp(-decay_rate)
    lam_re = radius * jnp.cos(mode_angle)
    lam_im = radius * jnp.sin(mode_angle)
    in_gain = jnp.sqrt(-jnp.expm1(-2.0 * decay_rate))
    return (decay_rate, radius, lam_re, lam_im, in_gain)

def record_grads(inputs, dilation, conv_w, skip_gain, w_in, w_out, lam_re, lam_im, in_gain):
    act_row, cot_row, keep_row = inputs
    length = act_row.shape[0]
    features = act_row.shape[1]
    mode_count = lam_re.shape[0]
    padded = jnp.concatenate([jnp.zeros((MAXLAG, features), act_row.dtype), act_row], axis=0)

    def tap_rows(k):
        start = (MAXLAG - dilation[k]).astype(jnp.int32)
        return lax.dynamic_slice_in_dim(padded, start, length, 0).astype(jnp.float32)
    conv_out = jnp.zeros((length, features), jnp.float32)
    for k in range(TAPS):
        conv_out = conv_out + conv_w[k] * tap_rows(k)
    conv_b = conv_out.astype(jnp.bfloat16)
    projected = jnp.dot(conv_b, w_in, preferred_element_type=jnp.float32)
    x_re = projected[:, :mode_count]
    x_im = projected[:, mode_count:]

    def forward_step(state_pair, step_in):
        old_re, old_im = state_pair
        keep_step, value_re, value_im = step_in
        new_re = keep_step * (lam_re * old_re - lam_im * old_im) + in_gain * value_re
        new_im = keep_step * (lam_im * old_re + lam_re * old_im) + in_gain * value_im
        return ((new_re, new_im), (new_re, new_im))
    zeros_row = jnp.zeros((mode_count,), jnp.float32)
    _, (h_re, h_im) = lax.scan(forward_step, (zeros_row, zeros_row), (keep_row, x_re, x_im))
    h_b = jnp.concatenate([h_re, h_im], axis=1).astype(jnp.bfloat16)
    raw_w_out = jnp.dot(h_b.T, cot_row, preferred_element_type=jnp.float32)
    back_proj = jnp.dot(cot_row, w_out.T, preferred_element_type=jnp.float32)
    e_re = back_proj[:, :mode_count]
    e_im = back_proj[:, mode_count:]
    keep_next = jnp.concatenate([keep_row[1:], jnp.ones((1,), jnp.float32)])

    def adjoint_step(state_pair, step_in):
        next_re, next_im = state_pair
        keep_step, value_re, value_im = step_in
        new_re = value_re + keep_step * (lam_re * next_re + lam_im * next_im)
        new_im = value_im + keep_step * (lam_re * next_im - lam_im * next_re)
        return ((new_re, new_im), (new_re, new_im))
    _, (delta_re, delta_im) = lax.scan(adjoint_step, (zeros_row, zeros_row), (keep_next, e_re, e_im), reverse=True)
    grad_x = jnp.concatenate([in_gain * delta_re, in_gain * delta_im], axis=1).astype(jnp.bfloat16)
    raw_w_in = jnp.dot(conv_b.T, grad_x, preferred_element_type=jnp.float32)
    cot_float = cot_row.astype(jnp.float32)
    grad_conv = jnp.dot(grad_x, w_in.T, preferred_element_type=jnp.float32) + skip_gain * cot_float
    raw_skip = lax.optimization_barrier(jnp.sum(cot_float * conv_out, axis=0))
    padded_grad = jnp.concatenate([grad_conv, jnp.zeros((MAXLAG, features), jnp.float32)], axis=0)
    grad_input = jnp.zeros((length, features), jnp.float32)
    tap_sums = []
    for k in range(TAPS):
        start = dilation[k].astype(jnp.int32)
        grad_input = grad_input + conv_w[k] * lax.dynamic_slice_in_dim(padded_grad, start, length, 0)
        tap_sums.append(lax.optimization_barrier(jnp.sum(grad_conv * tap_rows(k), axis=0)))
    raw_taps = jnp.stack(tap_sums)
    prev_re = jnp.concatenate([jnp.zeros((1, mode_count), jnp.float32), h_re[:-1]], axis=0)
    prev_im = jnp.concatenate([jnp.zeros((1, mode_count), jnp.float32), h_im[:-1]], axis=0)
    keep_col = keep_row[:, None]
    lam_grad_re = lax.optimization_barrier(jnp.sum(keep_col * (delta_re * prev_re + delta_im * prev_im), axis=0))
    lam_grad_im = lax.optimization_barrier(jnp.sum(keep_col * (delta_im * prev_re - delta_re * prev_im), axis=0))
    gain_grad = lax.optimization_barrier(jnp.sum(delta_re * x_re + delta_im * x_im, axis=0))
    return (grad_input.astype(jnp.bfloat16), raw_taps, raw_skip, raw_w_in, raw_w_out, lam_grad_re, lam_grad_im, gain_grad)

def reference(activations, cotangent, retain, dilation, conv_w, skip_gain, log_rate, mode_angle, w_in, w_out):
    decay_rate, radius, lam_re, lam_im, in_gain = decay_params(log_rate, mode_angle)
    per_record = partial(record_grads, dilation=dilation, conv_w=conv_w, skip_gain=skip_gain, w_in=w_in, w_out=w_out, lam_re=lam_re, lam_im=lam_im, in_gain=in_gain)
    results = lax.map(per_record, (activations, cotangent, retain))
    grad_input = results[0]
    raw_taps = lax.optimization_barrier(jnp.sum(results[1], axis=0))
    raw_skip = lax.optimization_barrier(jnp.sum(results[2], axis=0))
    raw_w_in = lax.optimization_barrier(jnp.sum(results[3], axis=0))
    raw_w_out = lax.optimization_barrier(jnp.sum(results[4], axis=0))
    lam_grad_re = lax.optimization_barrier(jnp.sum(results[5], axis=0))
    lam_grad_im = lax.optimization_barrier(jnp.sum(results[6], axis=0))
    gain_grad = lax.optimization_barrier(jnp.sum(results[7], axis=0))
    scale = 1.0 / math.sqrt(RECORDS * LEN)
    radius_grad = lam_grad_re * jnp.cos(mode_angle) + lam_grad_im * jnp.sin(mode_angle) - gain_grad * radius / in_gain
    grad_log_rate = -radius_grad * radius * decay_rate * scale
    grad_angle = (lam_grad_im * lam_re - lam_grad_re * lam_im) * scale
    return (grad_input, raw_taps * scale, raw_skip * scale, grad_log_rate, grad_angle, raw_w_in * scale, raw_w_out * scale)
```

```python
import functools
import math

import jax
import jax.numpy as jnp
from jax import lax
from jax.experimental import pallas as pl
from jax.experimental.pallas import tpu as pltpu
from jax.sharding import PartitionSpec as P

TAPS = 9
MAXLAG = 128
NB = 8
PIECE = 16
F32 = jnp.float32
BF16 = jnp.bfloat16


class Sizes:
    def __init__(self, tm, rec, time_steps, features, lag):
        self.core = 2
        self.nx = rec
        self.ny = 4 if tm >= 64 else 2
        self.nz = tm // (self.core * self.ny)
        self.group = self.core * self.ny
        self.recs = 2
        self.t = time_steps
        self.d = features
        self.lag = lag
        self.bl = time_steps // NB
        self.lw = features // 4
        self.half = features // 2
        self.xw = features // rec
        self.sw = features // self.ny
        self.chunk = min(64, time_steps)


def mul(ar, ai, br, bi):
    return ar * br - ai * bi, ar * bi + ai * br


def square_times(re, im, times):
    for _ in range(times):
        re, im = re * re - im * im, 2.0 * (re * im)
    return re, im


def log2(n):
    return n.bit_length() - 1


def kernel(
    s,
    dil_ref,
    retain_ref,
    convw_ref,
    par_ref,
    act_hbm,
    cot_hbm,
    win_hbm,
    wout_hbm,
    gin_ref,
    taps_ref,
    skip_ref,
    rate_ref,
    angle_ref,
    gwin_ref,
    gwout_ref,
    act_v,
    cot_v,
    win_v,
    wout_v,
    halo_v,
    ext_act,
    ext_grad,
    cotp_v,
    convb_v,
    convp_v,
    keep_v,
    e_v,
    x_v,
    hb_v,
    gx_v,
    head_v,
    ghalo_v,
    w1_v,
    w2_v,
    scan_a,
    scan_b,
    small_v,
    ssend,
    srecv_core,
    ssum_core,
    srecv_y,
    sx_v,
    sz_v,
    sall_v,
    send_w,
    recv_w,
    chip_w,
    recv1_w0,
    recv1_w1,
    sum1_w0,
    sum1_w1,
    recv2_w,
    sum2_w,
    recv3_w,
    full_w,
    in_sem,
    halo_sem,
    a_send,
    a_recv,
    b_send,
    b_recv,
    wc_sem,
    w1_send,
    w1_recv,
    w2_send,
    w2_recv,
    w3_send,
    w3_recv,
    w4_send,
    w4_recv,
    sc_sem,
    sy_send,
    sy_recv,
    sx_send,
    sx_recv,
    sz_send,
    sz_recv,
    sg_send,
    sg_recv,
    sf_sem,
):
    t_len, d, half, lw = s.t, s.d, s.half, s.lw
    tm = lax.axis_index("tm")
    rec = lax.axis_index("rec")
    core = lax.rem(tm, s.core)
    y = lax.rem(tm // s.core, s.ny)
    z = tm // s.group
    spot = lax.rem(tm, s.group)
    tm_count = s.nz * s.group
    other = 1 - core

    def at(tm_to, rec_to):
        return (tm_to, rec_to)

    def at_group(o):
        return at(z * s.group + lax.rem(spot + o, s.group), rec)

    def at_core():
        return at(tm + 1 - 2 * core, rec)

    def at_y(o):
        return at(z * s.group + lax.rem(y + o, s.ny) * s.core + core, rec)

    def at_z(o):
        return at(lax.rem(z + o, s.nz) * s.group + spot, rec)

    def at_x(o):
        return at(tm, lax.rem(rec + o, s.nx))

    def at_tm(o):
        return at(lax.rem(tm + o + tm_count, tm_count), rec)

    def remote(src, dst, ssem, rsem, to):
        return pltpu.make_async_remote_copy(
            src_ref=src,
            dst_ref=dst,
            send_sem=ssem,
            recv_sem=rsem,
            device_id=to,
            device_id_type=pl.DeviceIdType.MESH,
        )

    loads = [
        pltpu.make_async_copy(src, dst, in_sem.at[i])
        for i, (src, dst) in enumerate(
            ((cot_hbm, cot_v), (wout_hbm, wout_v), (act_hbm, act_v), (win_hbm, win_v))
        )
    ]
    for load in loads:
        load.start()
    scan_b[...] = jnp.zeros_like(scan_b)
    barrier = pltpu.get_barrier_semaphore()
    partners = (
        [at_group(o) for o in range(1, s.group)]
        + [at_z(o) for o in range(1, s.nz)]
        + [at_x(o) for o in range(1, s.nx)]
        + [at_tm(1), at_tm(-1)]
    )
    for partner in partners:
        pl.semaphore_signal(
            barrier, inc=1, device_id=partner, device_id_type=pl.DeviceIdType.MESH
        )

    row = lax.broadcasted_iota(jnp.int32, (t_len, t_len), 0)
    col = lax.broadcasted_iota(jnp.int32, (t_len, t_len), 1)
    chosen = col == lax.rem(row, NB) * s.bl + row // NB
    order = jnp.where(chosen, 1.0, 0.0).astype(BF16)
    for r in range(s.recs):
        picked = jnp.sum(
            jnp.where(chosen, retain_ref[r : r + 1, :], 0.0), axis=1, keepdims=True
        )
        keep_v[r] = jnp.broadcast_to(picked, (t_len, lw))

    lam_re = par_ref[0:1, :]
    lam_im = par_ref[1:2, :]
    in_gain = par_ref[2:3, :]
    block_pow = [square_times(lam_re, lam_im, log2(s.bl))]
    for _ in range(2):
        block_pow.append(square_times(*block_pow[-1], 1))
    dev_pow = square_times(*block_pow[-1], 1)
    plane_pow = square_times(*dev_pow, log2(s.group))

    def packed(v):
        pair = jnp.concatenate([v[:, :half], v[:, half:]], axis=0)
        return jnp.concatenate([pair] * s.recs, axis=0)

    dev_pack = (packed(dev_pow[0]), packed(dev_pow[1]))
    plane_pack = (packed(plane_pow[0]), packed(plane_pow[1]))
    sub_row = lax.broadcasted_iota(jnp.int32, (NB, d), 0)
    sub_row_k = lax.broadcasted_iota(jnp.int32, (NB, lw), 0)

    def power_table(index):
        re = jnp.ones((NB, d), F32)
        im = jnp.zeros((NB, d), F32)
        for bit, (pr, pi) in zip((1, 2, 4), block_pow):
            nr, ni = mul(re, im, pr, pi)
            here = lax.rem(index // bit, 2) == 1
            re = jnp.where(here, nr, re)
            im = jnp.where(here, ni, im)
        return re, im

    def wide(k):
        return jnp.concatenate([k] * (d // k.shape[1]), axis=1)

    def block_scan(e_re, e_im, k, sign):
        for span, (pr, pi) in zip((1, 2, 4), block_pow):
            shift = span if sign > 0 else NB - span
            pi = sign * pi
            n_re = pltpu.roll(e_re, shift, 0)
            n_im = pltpu.roll(e_im, shift, 0)
            n_k = pltpu.roll(k, shift, 0)
            there = sub_row >= span if sign > 0 else sub_row < NB - span
            there_k = sub_row_k >= span if sign > 0 else sub_row_k < NB - span
            m_re, m_im = mul(pr, pi, n_re, n_im)
            k_wide = wide(k)
            e_re = e_re + jnp.where(there, k_wide * m_re, 0.0)
            e_im = e_im + jnp.where(there, k_wide * m_im, 0.0)
            k = jnp.where(there_k, k * n_k, k)
        return e_re, e_im, k

    def summarize(way, scans):
        last = NB - 1 if way == 0 else 0
        for r in range(s.recs):
            e_re, e_im, k = scans[r]
            for part, v in enumerate((e_re, e_im)):
                for h in range(2):
                    at_row = part * 4 + r * 2 + h
                    scan_a[way, spot, at_row : at_row + 1, 0:half] = v[
                        last : last + 1, h * half : (h + 1) * half
                    ]
                    scan_a[way, spot, at_row : at_row + 1, half : half + lw] = k[
                        last : last + 1, :
                    ]

    def copy_a(way, o, back=False):
        held = scan_a.at[way, lax.rem(spot + s.group - o, s.group) if back else spot]
        return remote(held, held, a_send.at[way, o], a_recv.at[way, o], at_group(o))

    def copy_b(way, o, back=False):
        held = scan_b.at[way, lax.rem(z + s.nz - o, s.nz) if back else z]
        return remote(held, held, b_send.at[way, o], b_recv.at[way, o], at_z(o))

    def sends_b(way, o):
        return z + o < s.nz if way == 0 else z + o >= s.nz

    def gets_b(way, o):
        return z - o >= 0 if way == 0 else z - o < 0

    def start_a(way):
        for o in range(1, s.group):
            copy_a(way, o).start()

    def advance(slot, state, pack, way):
        sign = 1.0 if way == 0 else -1.0
        k = slot[0:4, half : half + lw]
        k = jnp.concatenate([k] * (half // lw), axis=1)
        m_re, m_im = mul(pack[0], sign * pack[1], state[0], state[1])
        return slot[0:4, 0:half] + k * m_re, slot[4:8, 0:half] + k * m_im

    def in_order(count, way):
        return range(count) if way == 0 else range(count - 1, -1, -1)

    def plane_step(way):
        for o in range(1, s.group):
            copy_a(way, o, True).wait_recv()
        state = (jnp.zeros((4, half), F32), jnp.zeros((4, half), F32))
        k_all = jnp.ones((4, lw), F32)
        for i in in_order(s.group, way):
            slot = scan_a[way, i]
            state = advance(slot, state, dev_pack, way)
            k_all = k_all * slot[0:4, half : half + lw]
        scan_b[way, z, 0:4, 0:half] = state[0]
        scan_b[way, z, 4:8, 0:half] = state[1]
        scan_b[way, z, 0:4, half : half + lw] = k_all
        scan_b[way, z, 4:8, half : half + lw] = k_all
        for o in range(1, s.nz):

            @pl.when(sends_b(way, o))
            def _():
                copy_b(way, o).start()

    def entering(way):
        for o in range(1, s.nz):

            @pl.when(gets_b(way, o))
            def _():
                copy_b(way, o, True).wait_recv()

        state = (jnp.zeros((4, half), F32), jnp.zeros((4, half), F32))
        for i in in_order(s.nz, way):
            moved = advance(scan_b[way, i], state, plane_pack, way)
            use = i < z if way == 0 else i > z
            state = tuple(jnp.where(use, m, o) for m, o in zip(moved, state))
        for i in in_order(s.group, way):
            moved = advance(scan_a[way, i], state, dev_pack, way)
            use = i < spot if way == 0 else i > spot
            state = tuple(jnp.where(use, m, o) for m, o in zip(moved, state))
        return state

    def block_entry(way, scans, state):
        sign = 1.0 if way == 0 else -1.0
        index = sub_row if way == 0 else NB - 1 - sub_row
        pw_re, pw_im = power_table(index)
        pw_im = sign * pw_im
        shift = 1 if way == 0 else NB - 1
        out = []
        for r in range(s.recs):
            s_re, s_im = (
                jnp.concatenate([v[2 * r : 2 * r + 1], v[2 * r + 1 : 2 * r + 2]], axis=1)
                for v in state
            )
            e_re, e_im, k = scans[r]
            m_re, m_im = mul(pw_re, pw_im, s_re, s_im)
            k_wide = wide(pltpu.roll(k, shift, 0))
            first = index == 0
            out.append(
                (
                    jnp.where(first, s_re, pltpu.roll(e_re, shift, 0) + k_wide * m_re),
                    jnp.where(first, s_im, pltpu.roll(e_im, shift, 0) + k_wide * m_im),
                )
            )
        return out

    lr = jnp.broadcast_to(lam_re, (NB, d))
    li = jnp.broadcast_to(lam_im, (NB, d))
    gain = jnp.broadcast_to(in_gain, (NB, d))
    zero = jnp.zeros((NB, d), F32)

    def rows(j):
        return pl.ds(pl.multiple_of(j * NB, NB), NB)

    def rows2(i):
        return pl.ds(pl.multiple_of(i * 2 * NB, 2 * NB), 2 * NB)

    loads[0].wait()
    loads[1].wait()
    nt = (((1,), (1,)), ((), ()))
    tn = (((0,), (0,)), ((), ()))
    for r in range(s.recs):
        cotp_v[r] = jnp.dot(order, cot_v[r], preferred_element_type=F32).astype(BF16)
        e_v[r] = lax.dot_general(cotp_v[r], wout_v[...], nt, preferred_element_type=F32)

    pl.semaphore_wait(barrier, len(partners))
    act_halo = remote(
        act_hbm.at[:, pl.ds(t_len - s.lag, s.lag), :],
        halo_v,
        halo_sem.at[0],
        halo_sem.at[1],
        at_tm(1),
    )
    act_halo.start()

    def adj_first(i, carry):
        j = s.bl - 1 - i
        new = []
        for r in range(s.recs):
            p_re, p_im, k_all = carry[r]
            k = keep_v[r, rows(j), :]
            k4 = wide(k)
            d_re = e_v[r, rows(j), 0:d] + p_re
            d_im = e_v[r, rows(j), d : 2 * d] + p_im
            m_re, m_im = mul(lr, -li, d_re, d_im)
            new.append((k4 * m_re, k4 * m_im, k_all * k))
        return tuple(new)

    ones_k = jnp.ones((NB, lw), F32)
    ends = lax.fori_loop(0, s.bl, adj_first, ((zero, zero, ones_k),) * s.recs)
    keeps = [ends[r][2] for r in range(s.recs)]
    adj_scans = [block_scan(*ends[r], -1.0) for r in range(s.recs)]
    summarize(1, adj_scans)
    start_a(1)

    loads[2].wait()
    for r in range(s.recs):
        for l in range(4):
            ext_act[r, l, s.lag : s.lag + t_len, :] = act_v[
                r, :, l * lw : (l + 1) * lw
            ].astype(F32)
    act_halo.wait_recv()
    for r in range(s.recs):
        for l in range(4):
            before = halo_v[r, :, l * lw : (l + 1) * lw].astype(F32)
            ext_act[r, l, 0 : s.lag, :] = jnp.where(tm > 0, before, 0.0)

    per_rec = t_len // s.chunk

    def fold(v):
        return jnp.sum(v.reshape(s.chunk // 8, 8, lw), axis=0)

    for l in range(4):
        lanes = slice(l * lw, (l + 1) * lw)
        taps_l = [convw_ref[k : k + 1, lanes] for k in range(TAPS)]

        def conv_step(i, acc):
            r = i // per_rec
            base = pl.multiple_of(lax.rem(i, per_rec) * s.chunk, s.chunk)
            out = jnp.zeros((s.chunk, lw), F32)
            for k in range(TAPS):
                out += taps_l[k] * ext_act[r, l, pl.ds(base + s.lag - dil_ref[k], s.chunk), :]
            convb_v[r, pl.ds(base, s.chunk), lanes] = out.astype(BF16)
            return acc + fold(out * cot_v[r, pl.ds(base, s.chunk), lanes].astype(F32))

        skip_acc = lax.fori_loop(0, s.recs * per_rec, conv_step, jnp.zeros((8, lw), F32))
        small_v[9:10, lanes] = jnp.sum(skip_acc, axis=0, keepdims=True)

    plane_step(1)

    loads[3].wait()
    for r in range(s.recs):
        convp_v[r] = jnp.dot(order, convb_v[r], preferred_element_type=F32).astype(BF16)
        x_v[r] = jnp.dot(convp_v[r], win_v[...], preferred_element_type=F32)

    def fwd_first(j, carry):
        new = []
        for r in range(s.recs):
            h_re, h_im = carry[r]
            k4 = wide(keep_v[r, rows(j), :])
            m_re, m_im = mul(lr, li, h_re, h_im)
            new.append(
                (
                    k4 * m_re + gain * x_v[r, rows(j), 0:d],
                    k4 * m_im + gain * x_v[r, rows(j), d : 2 * d],
                )
            )
        return tuple(new)

    ends = lax.fori_loop(0, s.bl, fwd_first, ((zero, zero),) * s.recs)
    fwd_scans = [block_scan(*ends[r], keeps[r], 1.0) for r in range(s.recs)]
    summarize(0, fwd_scans)
    start_a(0)

    entry = block_entry(1, adj_scans, entering(1))

    def adj_second(i, carry):
        i = s.bl // 2 - 1 - i
        new = []
        for r in range(s.recs):
            p_re, p_im = carry[r]
            held = [None, None]
            for sub in (1, 0):
                j = 2 * i + sub
                k4 = wide(keep_v[r, rows(j), :])
                d_re = e_v[r, rows(j), 0:d] + p_re
                d_im = e_v[r, rows(j), d : 2 * d] + p_im
                e_v[r, rows(j), 0:d] = d_re
                e_v[r, rows(j), d : 2 * d] = d_im
                held[sub] = (gain * d_re, gain * d_im)
                m_re, m_im = mul(lr, -li, d_re, d_im)
                p_re, p_im = k4 * m_re, k4 * m_im
            for part in range(2):
                gx_v[r, rows2(i), part * d : (part + 1) * d] = jnp.concatenate(
                    [held[0][part], held[1][part]], axis=0
                ).astype(BF16)
            new.append((p_re, p_im))
        return tuple(new)

    lax.fori_loop(0, s.bl // 2, adj_second, tuple(entry))

    plane_step(0)

    pieces = s.nz * s.ny

    def piece_in(g, c):
        at_row = pl.ds(pl.multiple_of((g * 2 + c) * 8, 8), 8)
        return jnp.concatenate([w1_v[at_row, 0:d], w1_v[at_row, d : 2 * d]], axis=0)

    def piece_out(g, c):
        return w2_v[pl.ds(pl.multiple_of((g * 2 + c) * PIECE, PIECE), PIECE), :]

    piece = (piece_in, piece_out)

    def core_copy(w):
        return remote(send_w.at[w], recv_w.at[w], wc_sem.at[w, 0], wc_sem.at[w, 1], at_core())

    def send_core(w):
        def one(g, _):
            send_w[w, g] = piece[w](g, other).astype(BF16)
            return 0

        lax.fori_loop(0, pieces, one, 0)
        core_copy(w).start()

    recv1 = (recv1_w0, recv1_w1)
    sum1 = (sum1_w0, sum1_w1)

    def copy1(w, o):
        if w == 0:
            src, to = chip_w.at[w, :, lax.rem(y + o, s.ny)], at_y(o)
        else:
            src, to = chip_w.at[w, lax.rem(rec + o, s.nx)], at_x(o)
        return remote(src, recv1[w].at[o - 1], w1_send.at[w, o], w1_recv.at[w, o], to)

    def copy2(w, o):
        if w == 0:
            src, to = sum1[w].at[lax.rem(rec + o, s.nx)], at_x(o)
        else:
            src, to = sum1[w].at[lax.rem(y + o, s.ny)], at_y(o)
        return remote(src, recv2_w.at[w, o - 1], w2_send.at[w, o], w2_recv.at[w, o], to)

    def copy3(w, o):
        src = sum2_w.at[w, lax.rem(z + o, s.nz)]
        return remote(src, recv3_w.at[w, o - 1], w3_send.at[w, o], w3_recv.at[w, o], at_z(o))

    def copy4(w, o, back=False):
        held = full_w.at[w, lax.rem(rec + s.nx - o, s.nx) if back else rec]
        return remote(held, held, w4_send.at[w, o], w4_recv.at[w, o], at_x(o))

    n1 = (s.ny, s.nx)
    n2 = (s.nx, s.ny)

    def stage1(w):
        core_copy(w).wait_recv()

        def one(g, _):
            total = piece[w](g, core) + recv_w[w, g].astype(F32)
            total = total.astype(BF16)
            for i in range(s.nx):
                chip_w[w, i, lax.rem(g, s.ny), g // s.ny] = total[:, i * s.xw : (i + 1) * s.xw]
            return 0

        lax.fori_loop(0, pieces, one, 0)
        for o in range(1, n1[w]):
            copy1(w, o).start()

    def stage2(w):
        for o in range(1, n1[w]):
            copy1(w, o).wait_recv()

        def one(i, _):
            own = chip_w[w, i, y] if w == 0 else chip_w[w, rec, i]
            total = own.astype(F32)
            for o in range(1, n1[w]):
                total += recv1[w][o - 1, i].astype(F32)
            sum1[w][i] = total.astype(BF16)
            return 0

        lax.fori_loop(0, n2[w], one, 0)
        for o in range(1, n2[w]):
            copy2(w, o).start()

    def stage3(w):
        for o in range(1, n2[w]):
            copy2(w, o).wait_recv()
        total = (sum1[w][rec] if w == 0 else sum1[w][y]).astype(F32)
        for o in range(1, n2[w]):
            total += recv2_w[w, o - 1].astype(F32)
        sum2_w[w] = total.astype(BF16)
        for o in range(1, s.nz):
            copy3(w, o).start()

    scale = 1.0 / math.sqrt(s.recs * s.nx * t_len * tm_count)

    def stage4(w):
        for o in range(1, s.nz):
            copy3(w, o).wait_recv()
        total = sum2_w[w, z].astype(F32)
        for o in range(1, s.nz):
            total += recv3_w[w, o - 1].astype(F32)
        full_w[w, rec] = total * scale
        for o in range(1, s.nx):
            copy4(w, o).start()

    def stage5(w):
        for o in range(1, s.nx):
            copy4(w, o, True).wait_recv()
        block = jnp.concatenate([full_w[w, i] for i in range(s.nx)], axis=1)
        if w == 0:
            gwin_ref[:, 0:d] = block[0:8]
            gwin_ref[:, d : 2 * d] = block[8:16]
        else:
            gwout_ref[...] = block

    total = jnp.zeros((d, 2 * d), F32)
    for r in range(s.recs):
        total += lax.dot_general(convp_v[r], gx_v[r], tn, preferred_element_type=F32)
    w1_v[...] = total
    send_core(0)

    for r in range(s.recs):
        gx_time = lax.dot_general(order, gx_v[r], tn, preferred_element_type=F32).astype(BF16)
        grad = lax.dot_general(gx_time, win_v[...], nt, preferred_element_type=F32)
        grad += par_ref[7:8, :] * cot_v[r].astype(F32)
        head_v[r] = grad[0 : s.lag, :].astype(BF16)
        for l in range(4):
            ext_grad[r, l, 0:t_len, :] = grad[:, l * lw : (l + 1) * lw]
    grad_halo = remote(head_v, ghalo_v, halo_sem.at[2], halo_sem.at[3], at_tm(-1))
    grad_halo.start()

    entry = block_entry(0, fwd_scans, entering(0))

    def fwd_second(i, carry):
        state, sums = carry
        new = []
        s_re, s_im, s_gain = sums
        for r in range(s.recs):
            h_re, h_im = state[r]
            held = [None, None]
            for sub in (0, 1):
                j = 2 * i + sub
                k4 = wide(keep_v[r, rows(j), :])
                kh_re, kh_im = k4 * h_re, k4 * h_im
                d_re = e_v[r, rows(j), 0:d]
                d_im = e_v[r, rows(j), d : 2 * d]
                x_re = x_v[r, rows(j), 0:d]
                x_im = x_v[r, rows(j), d : 2 * d]
                s_re += d_re * kh_re + d_im * kh_im
                s_im += d_im * kh_re - d_re * kh_im
                s_gain += d_re * x_re + d_im * x_im
                m_re, m_im = mul(lr, li, kh_re, kh_im)
                h_re = m_re + gain * x_re
                h_im = m_im + gain * x_im
                held[sub] = (h_re, h_im)
            for part in range(2):
                hb_v[r, rows2(i), part * d : (part + 1) * d] = jnp.concatenate(
                    [held[0][part], held[1][part]], axis=0
                ).astype(BF16)
            new.append((h_re, h_im))
        return tuple(new), (s_re, s_im, s_gain)

    _, sums = lax.fori_loop(0, s.bl // 2, fwd_second, (tuple(entry), (zero, zero, zero)))
    for i, v in enumerate(sums):
        small_v[10 + i : 11 + i, :] = jnp.sum(v, axis=0, keepdims=True)
    small_v[13:16, :] = jnp.zeros((3, d), F32)

    total = jnp.zeros((2 * d, d), F32)
    for r in range(s.recs):
        total += lax.dot_general(hb_v[r], cotp_v[r], tn, preferred_element_type=F32)
    w2_v[...] = total
    send_core(1)
    stage1(0)

    for l in range(4):
        lanes = slice(l * lw, (l + 1) * lw)

        def tap_step(i, acc):
            r = i // per_rec
            base = pl.multiple_of(lax.rem(i, per_rec) * s.chunk, s.chunk)
            grad = ext_grad[r, l, pl.ds(base, s.chunk), :]
            return tuple(
                acc[k]
                + fold(grad * ext_act[r, l, pl.ds(base + s.lag - dil_ref[k], s.chunk), :])
                for k in range(TAPS)
            )

        acc = lax.fori_loop(
            0, s.recs * per_rec, tap_step, (jnp.zeros((8, lw), F32),) * TAPS
        )
        for k in range(TAPS):
            small_v[k : k + 1, lanes] = jnp.sum(acc[k], axis=0, keepdims=True)

    for c in range(s.core):
        for i in range(s.ny):
            lane = (c * (s.ny // 2) + i // 2) * s.sw
            ssend[c, i] = small_v[(i % 2) * 8 : (i % 2) * 8 + 8, lane : lane + s.sw]
    small_core = remote(ssend.at[other], srecv_core, sc_sem.at[0], sc_sem.at[1], at_core())
    small_core.start()

    stage1(1)

    def copy_sy(o):
        to = lax.rem(y + o, s.ny)
        return remote(ssum_core.at[to], srecv_y.at[o - 1], sy_send.at[o], sy_recv.at[o], at_y(o))

    def copy_sx(o, back=False):
        held = sx_v.at[lax.rem(rec + s.nx - o, s.nx) if back else rec]
        return remote(held, held, sx_send.at[o], sx_recv.at[o], at_x(o))

    def copy_sz(o, back=False):
        held = sz_v.at[lax.rem(z + s.nz - o, s.nz) if back else z]
        return remote(held, held, sz_send.at[o], sz_recv.at[o], at_z(o))

    def copy_sg(o, back=False):
        held = sall_v.at[core, lax.rem(y + s.ny - o, s.ny) if back else y]
        return remote(held, held, sg_send.at[o], sg_recv.at[o], at_y(o))

    def copy_sf(back=False):
        held = sall_v.at[other if back else core]
        return remote(held, held, sf_sem.at[0], sf_sem.at[1], at_core())

    small_core.wait_recv()
    ssum_core[...] = ssend[core] + srecv_core[...]
    for o in range(1, s.ny):
        copy_sy(o).start()

    stage2(0)

    for o in range(1, s.ny):
        copy_sy(o).wait_recv()
    total = ssum_core[y]
    for o in range(1, s.ny):
        total += srecv_y[o - 1]
    sx_v[rec] = total
    for o in range(1, s.nx):
        copy_sx(o).start()

    stage2(1)

    for o in range(1, s.nx):
        copy_sx(o, True).wait_recv()
    total = sx_v[0]
    for i in range(1, s.nx):
        total += sx_v[i]
    sz_v[z] = total
    for o in range(1, s.nz):
        copy_sz(o).start()

    stage3(0)

    grad_halo.wait_recv()
    for r in range(s.recs):
        for l in range(4):
            after = ghalo_v[r, :, l * lw : (l + 1) * lw].astype(F32)
            ext_grad[r, l, t_len : t_len + s.lag, :] = jnp.where(tm < tm_count - 1, after, 0.0)
    for l in range(4):
        lanes = slice(l * lw, (l + 1) * lw)
        taps_l = [convw_ref[k : k + 1, lanes] for k in range(TAPS)]

        def grad_step(i, _):
            r = i // per_rec
            base = pl.multiple_of(lax.rem(i, per_rec) * s.chunk, s.chunk)
            out = jnp.zeros((s.chunk, lw), F32)
            for k in range(TAPS):
                out += taps_l[k] * ext_grad[r, l, pl.ds(base + dil_ref[k], s.chunk), :]
            gin_ref[r, pl.ds(base, s.chunk), lanes] = out.astype(BF16)
            return 0

        lax.fori_loop(0, s.recs * per_rec, grad_step, 0)

    for o in range(1, s.nz):
        copy_sz(o, True).wait_recv()
    total = sz_v[0]
    for i in range(1, s.nz):
        total += sz_v[i]
    sall_v[core, y] = total
    for o in range(1, s.ny):
        copy_sg(o).start()

    stage3(1)
    stage4(0)

    for o in range(1, s.ny):
        copy_sg(o, True).wait_recv()
    copy_sf().start()

    stage4(1)

    copy_sf(True).wait_recv()

    def small_rows(which):
        return jnp.concatenate(
            [
                sall_v[lane // (s.ny // 2), 2 * (lane % (s.ny // 2)) + which]
                for lane in range(d // s.sw)
            ],
            axis=1,
        )

    low, high = small_rows(0), small_rows(1)
    taps_ref[0:8, :] = low * scale
    taps_ref[8:9, :] = high[0:1] * scale
    skip_ref[...] = high[1:2] * scale
    lam_g_re, lam_g_im, gain_g = high[2:3], high[3:4], high[4:5]
    radius_grad = lam_g_re * par_ref[3:4, :] + lam_g_im * par_ref[4:5, :]
    radius_grad = radius_grad - gain_g * par_ref[5:6, :]
    rate_ref[...] = -radius_grad * par_ref[6:7, :] * scale
    angle_ref[...] = (lam_g_im * lam_re - lam_g_re * lam_im) * scale

    stage5(0)
    stage5(1)

    act_halo.wait_send()
    grad_halo.wait_send()
    for way in range(2):
        for o in range(1, s.group):
            copy_a(way, o).wait_send()
        for o in range(1, s.nz):

            @pl.when(sends_b(way, o))
            def _():
                copy_b(way, o).wait_send()

    for w in range(2):
        core_copy(w).wait_send()
        for o in range(1, n1[w]):
            copy1(w, o).wait_send()
        for o in range(1, n2[w]):
            copy2(w, o).wait_send()
        for o in range(1, s.nz):
            copy3(w, o).wait_send()
        for o in range(1, s.nx):
            copy4(w, o).wait_send()
    small_core.wait_send()
    for o in range(1, s.ny):
        copy_sy(o).wait_send()
        copy_sg(o).wait_send()
    for o in range(1, s.nx):
        copy_sx(o).wait_send()
    for o in range(1, s.nz):
        copy_sz(o).wait_send()
    copy_sf().wait_send()


def on_device(
    lag,
    activations,
    cotangent,
    retain,
    dilation,
    conv_w,
    skip_gain,
    log_rate,
    mode_angle,
    w_in,
    w_out,
):
    recs, time_steps, features = activations.shape
    s = Sizes(lax.axis_size("tm"), lax.axis_size("rec"), time_steps, features, lag)
    d, t = s.d, s.t
    decay_rate = jnp.exp(log_rate)
    radius = jnp.exp(-decay_rate)
    cos, sin = jnp.cos(mode_angle), jnp.sin(mode_angle)
    in_gain = jnp.sqrt(-jnp.expm1(-2.0 * decay_rate))
    params = jnp.stack(
        [
            radius * cos,
            radius * sin,
            in_gain,
            cos,
            sin,
            radius / in_gain,
            radius * decay_rate,
            skip_gain,
        ]
    )
    vmem = pl.BlockSpec(memory_space=pltpu.VMEM)
    smem = pl.BlockSpec(memory_space=pltpu.SMEM)
    hbm = pl.BlockSpec(memory_space=pl.ANY)
    pieces = s.nz * s.ny
    dma = pltpu.SemaphoreType.DMA
    buffers = [
        ((recs, t, d), BF16),
        ((recs, t, d), BF16),
        ((d, 2 * d), BF16),
        ((2 * d, d), BF16),
        ((recs, lag, d), BF16),
        ((recs, 4, t + lag, s.lw), F32),
        ((recs, 4, t + lag, s.lw), F32),
        ((recs, t, d), BF16),
        ((recs, t, d), BF16),
        ((recs, t, d), BF16),
        ((recs, t, s.lw), F32),
        ((recs, t, 2 * d), F32),
        ((recs, t, 2 * d), F32),
        ((recs, t, 2 * d), BF16),
        ((recs, t, 2 * d), BF16),
        ((recs, lag, d), BF16),
        ((recs, lag, d), BF16),
        ((d, 2 * d), F32),
        ((2 * d, d), F32),
        ((2, s.group, 8, s.half + s.lw), F32),
        ((2, s.nz, 8, s.half + s.lw), F32),
        ((16, d), F32),
        ((s.core, s.ny, 8, s.sw), F32),
        ((s.ny, 8, s.sw), F32),
        ((s.ny, 8, s.sw), F32),
        ((s.ny - 1, 8, s.sw), F32),
        ((s.nx, 8, s.sw), F32),
        ((s.nz, 8, s.sw), F32),
        ((s.core, s.ny, 8, s.sw), F32),
        ((2, pieces, PIECE, d), BF16),
        ((2, pieces, PIECE, d), BF16),
        ((2, s.nx, s.ny, s.nz, PIECE, s.xw), BF16),
        ((s.ny - 1, s.nx, s.nz, PIECE, s.xw), BF16),
        ((s.nx - 1, s.ny, s.nz, PIECE, s.xw), BF16),
        ((s.nx, s.nz, PIECE, s.xw), BF16),
        ((s.ny, s.nz, PIECE, s.xw), BF16),
        ((2, max(s.nx, s.ny) - 1, s.nz, PIECE, s.xw), BF16),
        ((2, s.nz, PIECE, s.xw), BF16),
        ((2, s.nz - 1, PIECE, s.xw), BF16),
        ((2, s.nx, PIECE, s.xw), F32),
    ]
    most = max(s.nx, s.ny)
    semaphores = [
        (4,),
        (4,),
        (2, s.group),
        (2, s.group),
        (2, s.nz),
        (2, s.nz),
        (2, 2),
        (2, most),
        (2, most),
        (2, most),
        (2, most),
        (2, s.nz),
        (2, s.nz),
        (2, s.nx),
        (2, s.nx),
        (2,),
        (s.ny,),
        (s.ny,),
        (s.nx,),
        (s.nx,),
        (s.nz,),
        (s.nz,),
        (s.ny,),
        (s.ny,),
        (2,),
    ]
    out = pl.pallas_call(
        functools.partial(kernel, s),
        out_shape=(
            jax.ShapeDtypeStruct((recs, t, d), BF16),
            jax.ShapeDtypeStruct((TAPS, d), F32),
            jax.ShapeDtypeStruct((1, d), F32),
            jax.ShapeDtypeStruct((1, d), F32),
            jax.ShapeDtypeStruct((1, d), F32),
            jax.ShapeDtypeStruct((8, 2 * d), F32),
            jax.ShapeDtypeStruct((16, d), F32),
        ),
        in_specs=[smem, vmem, vmem, vmem, hbm, hbm, hbm, hbm],
        out_specs=(vmem,) * 7,
        scratch_shapes=[pltpu.VMEM(shape, dtype) for shape, dtype in buffers]
        + [dma(shape) for shape in semaphores],
        compiler_params=pltpu.CompilerParams(
            collective_id=0, has_side_effects=True, vmem_limit_bytes=56 * 1024 * 1024
        ),
        cost_estimate=pl.CostEstimate(
            flops=2 * 5 * recs * t * d * 2 * d, bytes_accessed=6 << 20, transcendentals=0
        ),
    )(dilation, retain, conv_w, params, activations, cotangent, w_in, w_out)
    grad_input, taps, skip, rate, angle, grad_w_in, grad_w_out = out
    return (
        grad_input,
        taps,
        skip.reshape(d),
        rate.reshape(d),
        angle.reshape(d),
        grad_w_in,
        grad_w_out,
    )


def build(mesh, lag):
    wide = P("rec", "tm", None)
    return jax.shard_map(
        functools.partial(on_device, lag),
        mesh=mesh,
        in_specs=(wide, wide, P("rec", "tm")) + (P(),) * 7,
        out_specs=(wide, P(), P(), P(), P(), P("tm", None), P("tm", None)),
        check_vma=False,
    )


def solution(mesh):
    return build(mesh, MAXLAG)
```

```python
import functools
import math

import jax
import jax.numpy as jnp
from jax import lax
from jax.experimental import pallas as pl
from jax.experimental.pallas import tpu as pltpu
from jax.sharding import PartitionSpec as P

TAPS = 9
MAXLAG = 128
NB = 8
PIECE = 16
F32 = jnp.float32
BF16 = jnp.bfloat16


class Sizes:
    def __init__(self, tm, rec, time_steps, features, lag):
        self.core = 2
        self.nx = rec
        self.ny = 4 if tm >= 64 else 2
        self.nz = tm // (self.core * self.ny)
        self.group = self.core * self.ny
        self.recs = 2
        self.t = time_steps
        self.d = features
        self.lag = lag
        self.bl = time_steps // NB
        self.lw = features // 4
        self.half = features // 2
        self.xw = features // rec
        self.sw = 2 * features // self.group
        self.chunk = min(64, lag)
        self.hz = self.nz // 2


def mul(ar, ai, br, bi):
    return ar * br - ai * bi, ar * bi + ai * br


def square_times(re, im, times):
    for _ in range(times):
        re, im = re * re - im * im, 2.0 * (re * im)
    return re, im


def one_minus_exp(u):
    series = jnp.ones_like(u)
    for n in range(12, 1, -1):
        series = 1.0 - u * (1.0 / n) * series
    return jnp.where(u < 1.0, u * series, 1.0 - jnp.exp(-u))


def log2(n):
    return n.bit_length() - 1


def kernel(
    s,
    dil_ref,
    retain_ref,
    convw_ref,
    skip_ref,
    rate_ref,
    angle_ref,
    act_hbm,
    cot_hbm,
    win_hbm,
    wout_hbm,
    gin_hbm,
    packed_ref,
    act_v,
    cot_v,
    win_v,
    wout_v,
    halo_v,
    ext_act,
    ext_grad,
    cotp_v,
    convb_v,
    convp_v,
    keep_v,
    e_v,
    x_v,
    hb_v,
    gx_v,
    head_v,
    ghalo_v,
    gin_v,
    w1_v,
    w2_v,
    scan_a,
    scan_b,
    small_v,
    skip_v,
    ssend,
    srecv,
    sx_v,
    sz_v,
    sall_v,
    send_w,
    recv_w,
    in_chip,
    in_recv1,
    in_sum1,
    in_recv2,
    in_sum2,
    in_recv3,
    in_full,
    out_chip,
    out_recv1,
    out_sum1,
    out_recv2,
    out_x,
    in_sem,
    halo_sem,
    ghalo_sem,
    gin_sem,
    a_send,
    a_recv,
    b_send,
    b_recv,
    wc_sem,
    i1_send,
    i1_recv,
    i2_send,
    i2_recv,
    i3_send,
    i3_recv,
    i4_send,
    i4_recv,
    o1_send,
    o1_recv,
    o2_send,
    o2_recv,
    o3_send,
    o3_recv,
    sr_send,
    sr_recv,
    sx_send,
    sx_recv,
    sz_send,
    sz_recv,
    sg_send,
    sg_recv,
):
    t_len, d, half, lw = s.t, s.d, s.half, s.lw
    tm = lax.axis_index("tm")
    rec = lax.axis_index("rec")
    core = lax.rem(tm, s.core)
    y = lax.rem(tm // s.core, s.ny)
    z = tm // s.group
    spot = lax.rem(tm, s.group)
    tm_count = s.nz * s.group
    other = 1 - core

    def at(tm_to, rec_to):
        return (tm_to, rec_to)

    def at_group(o):
        return at(z * s.group + lax.rem(spot + o, s.group), rec)

    def at_core():
        return at(tm + 1 - 2 * core, rec)

    def at_y(o):
        return at(z * s.group + lax.rem(y + o, s.ny) * s.core + core, rec)

    def at_z(o):
        return at(lax.rem(z + o, s.nz) * s.group + spot, rec)

    def at_x(o):
        return at(tm, lax.rem(rec + o, s.nx))

    def at_tm(o):
        return at(lax.rem(tm + o + tm_count, tm_count), rec)

    def remote(src, dst, ssem, rsem, to):
        return pltpu.make_async_remote_copy(
            src_ref=src,
            dst_ref=dst,
            send_sem=ssem,
            recv_sem=rsem,
            device_id=to,
            device_id_type=pl.DeviceIdType.MESH,
        )

    loads = [
        pltpu.make_async_copy(src, dst, in_sem.at[i])
        for i, (src, dst) in enumerate(
            ((cot_hbm, cot_v), (wout_hbm, wout_v), (act_hbm, act_v), (win_hbm, win_v))
        )
    ]
    barrier = pltpu.get_barrier_semaphore()
    partners = (
        [at_group(o) for o in range(1, s.group)]
        + [at_z(o) for o in range(1, s.nz)]
        + [at_x(o) for o in range(1, s.nx)]
        + [at_tm(1), at_tm(-1)]
    )
    for partner in partners:
        pl.semaphore_signal(
            barrier, inc=1, device_id=partner, device_id_type=pl.DeviceIdType.MESH
        )
    for load in loads:
        load.start()
    pl.semaphore_wait(barrier, len(partners))

    def act_halo(r):
        return remote(
            act_hbm.at[r, pl.ds(t_len - s.lag, s.lag), :],
            halo_v.at[r],
            halo_sem.at[r, 0],
            halo_sem.at[r, 1],
            at_tm(1),
        )

    for r in range(s.recs):
        act_halo(r).start()

    row = lax.broadcasted_iota(jnp.int32, (t_len, t_len), 0)
    col = lax.broadcasted_iota(jnp.int32, (t_len, t_len), 1)
    chosen = col == lax.rem(row, NB) * s.bl + row // NB
    order = jnp.where(chosen, 1.0, 0.0).astype(BF16)
    for r in range(s.recs):
        picked = jnp.sum(
            jnp.where(chosen, retain_ref[r : r + 1, :], 0.0), axis=1, keepdims=True
        )
        keep_v[r] = jnp.broadcast_to(picked, (t_len, lw))

    decay_rate = jnp.exp(rate_ref[...])
    radius = jnp.exp(-decay_rate)
    cos, sin = jnp.cos(angle_ref[...]), jnp.sin(angle_ref[...])
    lam_re = radius * cos
    lam_im = radius * sin
    in_gain = jnp.sqrt(one_minus_exp(2.0 * decay_rate))
    block_pow = [square_times(lam_re, lam_im, log2(s.bl))]
    for _ in range(2):
        block_pow.append(square_times(*block_pow[-1], 1))
    dev_pow = square_times(*block_pow[-1], 1)
    plane_pow = square_times(*dev_pow, log2(s.group))

    def packed(v):
        pair = jnp.concatenate([v[:, :half], v[:, half:]], axis=0)
        return jnp.concatenate([pair] * s.recs, axis=0)

    dev_pack = (packed(dev_pow[0]), packed(dev_pow[1]))
    plane_pack = (packed(plane_pow[0]), packed(plane_pow[1]))
    sub_row = lax.broadcasted_iota(jnp.int32, (NB, d), 0)
    sub_row_k = lax.broadcasted_iota(jnp.int32, (NB, lw), 0)

    def power_table(index):
        re = jnp.ones((NB, d), F32)
        im = jnp.zeros((NB, d), F32)
        for bit, (pr, pi) in zip((1, 2, 4), block_pow):
            nr, ni = mul(re, im, pr, pi)
            here = lax.rem(index // bit, 2) == 1
            re = jnp.where(here, nr, re)
            im = jnp.where(here, ni, im)
        return re, im

    def wide(k):
        return jnp.concatenate([k] * (d // k.shape[1]), axis=1)

    def block_scan(e_re, e_im, k, sign):
        for span, (pr, pi) in zip((1, 2, 4), block_pow):
            shift = span if sign > 0 else NB - span
            pi = sign * pi
            n_re = pltpu.roll(e_re, shift, 0)
            n_im = pltpu.roll(e_im, shift, 0)
            n_k = pltpu.roll(k, shift, 0)
            there = sub_row >= span if sign > 0 else sub_row < NB - span
            there_k = sub_row_k >= span if sign > 0 else sub_row_k < NB - span
            m_re, m_im = mul(pr, pi, n_re, n_im)
            k_wide = wide(k)
            e_re = e_re + jnp.where(there, k_wide * m_re, 0.0)
            e_im = e_im + jnp.where(there, k_wide * m_im, 0.0)
            k = jnp.where(there_k, k * n_k, k)
        return e_re, e_im, k

    def summarize(way, scans):
        last = NB - 1 if way == 0 else 0
        for r in range(s.recs):
            e_re, e_im, k = scans[r]
            for part, v in enumerate((e_re, e_im)):
                for h in range(2):
                    at_row = part * 4 + r * 2 + h
                    scan_a[way, spot, at_row : at_row + 1, 0:half] = v[
                        last : last + 1, h * half : (h + 1) * half
                    ]
                    scan_a[way, spot, at_row : at_row + 1, half : half + lw] = k[
                        last : last + 1, :
                    ]

    def copy_a(way, o, back=False):
        held = scan_a.at[way, lax.rem(spot + s.group - o, s.group) if back else spot]
        return remote(held, held, a_send.at[way, o], a_recv.at[way, o], at_group(o))

    def copy_b(way, o, back=False):
        held = scan_b.at[way, lax.rem(z + s.nz - o, s.nz) if back else z]
        return remote(held, held, b_send.at[way, o], b_recv.at[way, o], at_z(o))

    def sends_b(way, o):
        return z + o < s.nz if way == 0 else z + o >= s.nz

    def gets_b(way, o):
        return z - o >= 0 if way == 0 else z - o < 0

    def start_a(way):
        for o in range(1, s.group):
            copy_a(way, o).start()

    def advance(slot, state, pack, way):
        sign = 1.0 if way == 0 else -1.0
        k = slot[0:4, half : half + lw]
        k = jnp.concatenate([k] * (half // lw), axis=1)
        m_re, m_im = mul(pack[0], sign * pack[1], state[0], state[1])
        return slot[0:4, 0:half] + k * m_re, slot[4:8, 0:half] + k * m_im

    def in_order(count, way):
        return range(count) if way == 0 else range(count - 1, -1, -1)

    def plane_step(way):
        for o in range(1, s.group):
            copy_a(way, o, True).wait_recv()
        state = (jnp.zeros((4, half), F32), jnp.zeros((4, half), F32))
        k_all = jnp.ones((4, lw), F32)
        for i in in_order(s.group, way):
            slot = scan_a[way, i]
            state = advance(slot, state, dev_pack, way)
            k_all = k_all * slot[0:4, half : half + lw]
        scan_b[way, z, 0:4, 0:half] = state[0]
        scan_b[way, z, 4:8, 0:half] = state[1]
        scan_b[way, z, 0:4, half : half + lw] = k_all
        scan_b[way, z, 4:8, half : half + lw] = k_all
        for o in range(1, s.nz):

            @pl.when(sends_b(way, o))
            def _():
                copy_b(way, o).start()

    def entering(way):
        for o in range(1, s.nz):

            @pl.when(gets_b(way, o))
            def _():
                copy_b(way, o, True).wait_recv()

        state = (jnp.zeros((4, half), F32), jnp.zeros((4, half), F32))
        for i in in_order(s.nz, way):
            moved = advance(scan_b[way, i], state, plane_pack, way)
            use = i < z if way == 0 else i > z
            state = tuple(jnp.where(use, m, o) for m, o in zip(moved, state))
        for i in in_order(s.group, way):
            moved = advance(scan_a[way, i], state, dev_pack, way)
            use = i < spot if way == 0 else i > spot
            state = tuple(jnp.where(use, m, o) for m, o in zip(moved, state))
        return state

    def block_entry(way, scans, state):
        sign = 1.0 if way == 0 else -1.0
        index = sub_row if way == 0 else NB - 1 - sub_row
        pw_re, pw_im = power_table(index)
        pw_im = sign * pw_im
        shift = 1 if way == 0 else NB - 1
        out = []
        for r in range(s.recs):
            s_re, s_im = (
                jnp.concatenate([v[2 * r : 2 * r + 1], v[2 * r + 1 : 2 * r + 2]], axis=1)
                for v in state
            )
            e_re, e_im, k = scans[r]
            m_re, m_im = mul(pw_re, pw_im, s_re, s_im)
            k_wide = wide(pltpu.roll(k, shift, 0))
            first = index == 0
            out.append(
                (
                    jnp.where(first, s_re, pltpu.roll(e_re, shift, 0) + k_wide * m_re),
                    jnp.where(first, s_im, pltpu.roll(e_im, shift, 0) + k_wide * m_im),
                )
            )
        return out

    lr = jnp.broadcast_to(lam_re, (NB, d))
    li = jnp.broadcast_to(lam_im, (NB, d))
    gain = jnp.broadcast_to(in_gain, (NB, d))
    zero = jnp.zeros((NB, d), F32)

    def rows(j):
        return pl.ds(pl.multiple_of(j * NB, NB), NB)

    def rows2(i):
        return pl.ds(pl.multiple_of(i * 2 * NB, 2 * NB), 2 * NB)

    loads[0].wait()
    loads[1].wait()
    nt = (((1,), (1,)), ((), ()))
    tn = (((0,), (0,)), ((), ()))
    for r in range(s.recs):
        cotp_v[r] = jnp.dot(order, cot_v[r], preferred_element_type=F32).astype(BF16)
        e_v[r] = lax.dot_general(cotp_v[r], wout_v[...], nt, preferred_element_type=F32)

    def adj_first(i, carry):
        j = s.bl - 1 - i
        new = []
        for r in range(s.recs):
            p_re, p_im, k_all = carry[r]
            k = keep_v[r, rows(j), :]
            k4 = wide(k)
            d_re = e_v[r, rows(j), 0:d] + p_re
            d_im = e_v[r, rows(j), d : 2 * d] + p_im
            m_re, m_im = mul(lr, -li, d_re, d_im)
            new.append((k4 * m_re, k4 * m_im, k_all * k))
        return tuple(new)

    ones_k = jnp.ones((NB, lw), F32)
    ends = lax.fori_loop(0, s.bl, adj_first, ((zero, zero, ones_k),) * s.recs, unroll=4)
    keeps = [ends[r][2] for r in range(s.recs)]
    adj_scans = [block_scan(*ends[r], -1.0) for r in range(s.recs)]
    summarize(1, adj_scans)
    start_a(1)

    loads[2].wait()
    for r in range(s.recs):
        for l in range(4):
            ext_act[r, l, s.lag : s.lag + t_len, :] = act_v[
                r, :, l * lw : (l + 1) * lw
            ].astype(F32)
    per_rec = t_len // s.chunk

    def fold(v):
        return jnp.sum(v.reshape(s.chunk // 8, 8, lw), axis=0)

    def conv_block(l, r, base):
        lanes = slice(l * lw, (l + 1) * lw)
        base = pl.multiple_of(base, s.chunk)
        out = jnp.zeros((s.chunk, lw), F32)
        for k in range(TAPS):
            shifted = ext_act[r, l, pl.ds(base + s.lag - dil_ref[k], s.chunk), :]
            out += convw_ref[k : k + 1, lanes] * shifted
        convb_v[r, pl.ds(base, s.chunk), lanes] = out.astype(BF16)
        return fold(out * cot_v[r, pl.ds(base, s.chunk), lanes].astype(F32))

    low_chunks = s.lag // s.chunk
    high_chunks = per_rec - low_chunks
    none = jnp.zeros((8, lw), F32)
    for l in range(4):

        def high_step(i, acc):
            base = s.lag + lax.rem(i, high_chunks) * s.chunk
            return acc + conv_block(l, i // high_chunks, base)

        acc = lax.fori_loop(0, s.recs * high_chunks, high_step, none, unroll=2)
        skip_v[:, l * lw : (l + 1) * lw] = acc

    plane_step(1)

    loads[3].wait()
    for r in range(s.recs):
        act_halo(r).wait_recv()
        for l in range(4):
            lanes = slice(l * lw, (l + 1) * lw)
            before = halo_v[r, :, lanes].astype(F32)
            ext_act[r, l, 0 : s.lag, :] = jnp.where(tm > 0, before, 0.0)

            def low_step(i, acc):
                return acc + conv_block(l, r, i * s.chunk)

            skip_v[:, lanes] += lax.fori_loop(0, low_chunks, low_step, none, unroll=2)
        convp_v[r] = jnp.dot(order, convb_v[r], preferred_element_type=F32).astype(BF16)
        x_v[r] = jnp.dot(convp_v[r], win_v[...], preferred_element_type=F32)

    def fwd_first(j, carry):
        new = []
        for r in range(s.recs):
            h_re, h_im = carry[r]
            k4 = wide(keep_v[r, rows(j), :])
            m_re, m_im = mul(lr, li, h_re, h_im)
            new.append(
                (
                    k4 * m_re + x_v[r, rows(j), 0:d],
                    k4 * m_im + x_v[r, rows(j), d : 2 * d],
                )
            )
        return tuple(new)

    ends = lax.fori_loop(0, s.bl, fwd_first, ((zero, zero),) * s.recs, unroll=4)
    fwd_scans = [block_scan(*ends[r], keeps[r], 1.0) for r in range(s.recs)]
    summarize(0, fwd_scans)
    start_a(0)

    entry = block_entry(1, adj_scans, entering(1))

    def adj_second(i, carry):
        i = s.bl // 2 - 1 - i
        new = []
        for r in range(s.recs):
            p_re, p_im = carry[r]
            held = [None, None]
            for sub in (1, 0):
                j = 2 * i + sub
                k4 = wide(keep_v[r, rows(j), :])
                d_re = e_v[r, rows(j), 0:d] + p_re
                d_im = e_v[r, rows(j), d : 2 * d] + p_im
                e_v[r, rows(j), 0:d] = d_re
                e_v[r, rows(j), d : 2 * d] = d_im
                held[sub] = (gain * d_re, gain * d_im)
                m_re, m_im = mul(lr, -li, d_re, d_im)
                p_re, p_im = k4 * m_re, k4 * m_im
            for part in range(2):
                gx_v[r, rows2(i), part * d : (part + 1) * d] = jnp.concatenate(
                    [held[0][part], held[1][part]], axis=0
                ).astype(BF16)
            new.append((p_re, p_im))
        return tuple(new)

    lax.fori_loop(0, s.bl // 2, adj_second, tuple(entry), unroll=2)

    pieces = s.nz * s.ny
    part = pieces // 2

    def piece_in(g, c):
        at_row = pl.ds(pl.multiple_of((g * 2 + c) * 8, 8), 8)
        return jnp.concatenate([w1_v[at_row, 0:d], w1_v[at_row, d : 2 * d]], axis=0)

    def piece_out(g, c):
        return w2_v[pl.ds(pl.multiple_of((g * 2 + c) * PIECE, PIECE), PIECE), :]

    piece = (piece_in, piece_out)

    def core_copy(w, p):
        some = pl.ds(p * part, part)
        return remote(
            send_w.at[w, some],
            recv_w.at[w, some],
            wc_sem.at[w, p, 0],
            wc_sem.at[w, p, 1],
            at_core(),
        )

    def send_core(w, p):
        def one(g, _):
            send_w[w, g] = piece[w](g, other).astype(BF16)
            return 0

        lax.fori_loop(p * part, (p + 1) * part, one, 0, unroll=2)
        core_copy(w, p).start()

    def chip_sum(w, g):
        return (piece[w](g, core) + recv_w[w, g].astype(F32)).astype(BF16)

    def in_copy1(o):
        src = in_chip.at[lax.rem(rec + o, s.nx)]
        return remote(src, in_recv1.at[o - 1], i1_send.at[o], i1_recv.at[o], at_x(o))

    def in_copy2(o):
        src = in_sum1.at[lax.rem(y + o, s.ny)]
        return remote(src, in_recv2.at[o - 1], i2_send.at[o], i2_recv.at[o], at_y(o))

    def in_copy3(o):
        src = in_sum2.at[lax.rem(z + o, s.nz)]
        return remote(src, in_recv3.at[o - 1], i3_send.at[o], i3_recv.at[o], at_z(o))

    def in_copy4(o, back=False):
        held = in_full.at[lax.rem(rec + s.nx - o, s.nx) if back else rec]
        return remote(held, held, i4_send.at[o], i4_recv.at[o], at_x(o))

    def in_stage1():
        for p in range(2):
            core_copy(0, p).wait_recv()

        def one(g, _):
            total = chip_sum(0, g)
            for i in range(s.nx):
                in_chip[i, lax.rem(g, s.ny), g // s.ny] = total[:, i * s.xw : (i + 1) * s.xw]
            return 0

        lax.fori_loop(0, pieces, one, 0, unroll=4)
        for o in range(1, s.nx):
            in_copy1(o).start()

    def in_stage2():
        for o in range(1, s.nx):
            in_copy1(o).wait_recv()

        def one(i, _):
            total = in_chip[rec, i].astype(F32)
            for o in range(1, s.nx):
                total += in_recv1[o - 1, i].astype(F32)
            in_sum1[i] = total.astype(BF16)
            return 0

        lax.fori_loop(0, s.ny, one, 0)
        for o in range(1, s.ny):
            in_copy2(o).start()

    def in_stage3():
        for o in range(1, s.ny):
            in_copy2(o).wait_recv()
        total = in_sum1[y].astype(F32)
        for o in range(1, s.ny):
            total += in_recv2[o - 1].astype(F32)
        in_sum2[...] = total.astype(BF16)
        for o in range(1, s.nz):
            in_copy3(o).start()

    scale = 1.0 / math.sqrt(s.recs * s.nx * t_len * tm_count)

    def in_stage4():
        for o in range(1, s.nz):
            in_copy3(o).wait_recv()
        total = in_sum2[z].astype(F32)
        for o in range(1, s.nz):
            total += in_recv3[o - 1].astype(F32)
        in_full[rec] = total * scale
        for o in range(1, s.nx):
            in_copy4(o).start()

    def in_stage5():
        for o in range(1, s.nx):
            in_copy4(o, True).wait_recv()
        block = jnp.concatenate([in_full[i] for i in range(s.nx)], axis=1)
        packed_ref[16:32, :] = block

    def out_copy1(p, o):
        some = pl.ds(p * s.hz, s.hz)
        return remote(
            out_chip.at[lax.rem(y + o, s.ny), some],
            out_recv1.at[o - 1, some],
            o1_send.at[p, o],
            o1_recv.at[p, o],
            at_y(o),
        )

    def out_copy2(to):
        return remote(
            out_sum1.at[to],
            out_recv2.at[z],
            o2_send.at[to],
            o2_recv.at[z],
            at(to * s.group + spot, rec),
        )

    def out_from2(z_from):
        held = out_recv2.at[z_from]
        return remote(
            held, held, o2_send.at[z_from], o2_recv.at[z_from], at(z_from * s.group + spot, rec)
        )

    def out_copy3(o, back=False):
        held = out_x.at[lax.rem(rec + s.nx - o, s.nx) if back else rec]
        return remote(held, held, o3_send.at[o], o3_recv.at[o], at_x(o))

    def out_stage1(p):
        core_copy(1, p).wait_recv()

        def one(g, _):
            out_chip[lax.rem(g, s.ny), g // s.ny] = chip_sum(1, g)
            return 0

        lax.fori_loop(p * part, (p + 1) * part, one, 0, unroll=2)
        for o in range(1, s.ny):
            out_copy1(p, o).start()

    def out_stage2(p):
        for o in range(1, s.ny):
            out_copy1(p, o).wait_recv()
        for i in range(p * s.hz, (p + 1) * s.hz):
            total = out_chip[y, i].astype(F32)
            for o in range(1, s.ny):
                total += out_recv1[o - 1, i].astype(F32)
            out_sum1[i] = total.astype(BF16)

            @pl.when(i != z)
            def _():
                out_copy2(i).start()

    def out_stage3():
        for i in range(s.nz):

            @pl.when(i != z)
            def _():
                out_from2(i).wait_recv()

        out_recv2[z] = out_sum1[z]
        total = out_recv2[0].astype(F32)
        for i in range(1, s.nz):
            total += out_recv2[i].astype(F32)
        out_x[rec] = total.astype(BF16)
        for o in range(1, s.nx):
            out_copy3(o).start()

    def out_stage4():
        for o in range(1, s.nx):
            out_copy3(o, True).wait_recv()
        total = out_x[0].astype(F32)
        for i in range(1, s.nx):
            total += out_x[i].astype(F32)
        packed_ref[32:48, :] = total * scale

    half_d = d // 2
    for p in range(2):
        total = jnp.zeros((half_d, 2 * d), F32)
        for r in range(s.recs):
            total += lax.dot_general(
                convp_v[r, :, p * half_d : (p + 1) * half_d],
                gx_v[r],
                tn,
                preferred_element_type=F32,
            )
        w1_v[p * half_d : (p + 1) * half_d, :] = total
        send_core(0, p)

    plane_step(0)

    def grad_halo(r):
        return remote(
            head_v.at[r], ghalo_v.at[r], ghalo_sem.at[r, 0], ghalo_sem.at[r, 1], at_tm(-1)
        )

    for r in range(s.recs):
        gx_time = lax.dot_general(order, gx_v[r], tn, preferred_element_type=F32).astype(BF16)
        grad = lax.dot_general(gx_time, win_v[...], nt, preferred_element_type=F32)
        grad += skip_ref[...] * cot_v[r].astype(F32)
        head_v[r] = grad[0 : s.lag, :].astype(BF16)
        for l in range(4):
            ext_grad[r, l, 0:t_len, :] = grad[:, l * lw : (l + 1) * lw]
        grad_halo(r).start()

    in_stage1()

    for l in range(4):
        lanes = slice(l * lw, (l + 1) * lw)

        def tap_step(i, acc):
            r = i // per_rec
            base = pl.multiple_of(lax.rem(i, per_rec) * s.chunk, s.chunk)
            grad = ext_grad[r, l, pl.ds(base, s.chunk), :]
            return tuple(
                acc[k]
                + fold(grad * ext_act[r, l, pl.ds(base + s.lag - dil_ref[k], s.chunk), :])
                for k in range(TAPS)
            )

        acc = lax.fori_loop(0, s.recs * per_rec, tap_step, (none,) * TAPS, unroll=2)
        for k in range(TAPS):
            small_v[k : k + 1, lanes] = jnp.sum(acc[k], axis=0, keepdims=True)
    small_v[9:10, :] = jnp.sum(skip_v[...], axis=0, keepdims=True)

    entry = block_entry(0, fwd_scans, entering(0))

    def fwd_second(i, carry):
        state, sums = carry
        new = []
        s_re, s_im, s_gain = sums
        for r in range(s.recs):
            h_re, h_im = state[r]
            held = [None, None]
            for sub in (0, 1):
                j = 2 * i + sub
                k4 = wide(keep_v[r, rows(j), :])
                kh_re, kh_im = k4 * h_re, k4 * h_im
                d_re = e_v[r, rows(j), 0:d]
                d_im = e_v[r, rows(j), d : 2 * d]
                x_re = x_v[r, rows(j), 0:d]
                x_im = x_v[r, rows(j), d : 2 * d]
                s_re += d_re * kh_re + d_im * kh_im
                s_im += d_im * kh_re - d_re * kh_im
                s_gain += d_re * x_re + d_im * x_im
                m_re, m_im = mul(lr, li, kh_re, kh_im)
                h_re = m_re + x_re
                h_im = m_im + x_im
                held[sub] = (gain * h_re, gain * h_im)
            for part in range(2):
                hb_v[r, rows2(i), part * d : (part + 1) * d] = jnp.concatenate(
                    [held[0][part], held[1][part]], axis=0
                ).astype(BF16)
            new.append((h_re, h_im))
        return tuple(new), (s_re, s_im, s_gain)

    _, sums = lax.fori_loop(
        0, s.bl // 2, fwd_second, (tuple(entry), (zero, zero, zero)), unroll=2
    )
    for p in range(2):
        total = jnp.zeros((d, d), F32)
        for r in range(s.recs):
            total += lax.dot_general(
                hb_v[r, :, p * d : (p + 1) * d], cotp_v[r], tn, preferred_element_type=F32
            )
        w2_v[p * d : (p + 1) * d, :] = total
        send_core(1, p)

    sums = (in_gain * sums[0], in_gain * sums[1], sums[2])
    for i, v in enumerate(sums):
        small_v[10 + i : 11 + i, :] = jnp.sum(v, axis=0, keepdims=True)
    small_v[13:16, :] = jnp.zeros((3, d), F32)

    for i in range(s.group):
        lane = (i // 2) * s.sw
        ssend[i] = small_v[(i % 2) * 8 : (i % 2) * 8 + 8, lane : lane + s.sw]

    def copy_sr(o):
        src = ssend.at[lax.rem(spot + o, s.group)]
        return remote(src, srecv.at[o - 1], sr_send.at[o], sr_recv.at[o], at_group(o))

    def copy_sx(o, back=False):
        held = sx_v.at[lax.rem(rec + s.nx - o, s.nx) if back else rec]
        return remote(held, held, sx_send.at[o], sx_recv.at[o], at_x(o))

    def copy_sz(o, back=False):
        held = sz_v.at[lax.rem(z + s.nz - o, s.nz) if back else z]
        return remote(held, held, sz_send.at[o], sz_recv.at[o], at_z(o))

    def copy_sg(o, back=False):
        held = sall_v.at[lax.rem(spot + s.group - o, s.group) if back else spot]
        return remote(held, held, sg_send.at[o], sg_recv.at[o], at_group(o))

    for o in range(1, s.group):
        copy_sr(o).start()

    out_stage1(0)
    out_stage1(1)

    for o in range(1, s.group):
        copy_sr(o).wait_recv()
    total = ssend[spot]
    for o in range(1, s.group):
        total += srecv[o - 1]
    sx_v[rec] = total
    for o in range(1, s.nx):
        copy_sx(o).start()

    in_stage2()

    for r in range(s.recs):
        grad_halo(r).wait_recv()
        for l in range(4):
            after = ghalo_v[r, :, l * lw : (l + 1) * lw].astype(F32)
            ext_grad[r, l, t_len : t_len + s.lag, :] = jnp.where(tm < tm_count - 1, after, 0.0)
    for l in range(4):
        lanes = slice(l * lw, (l + 1) * lw)
        taps_l = [convw_ref[k : k + 1, lanes] for k in range(TAPS)]

        def grad_step(i, _):
            r = i // per_rec
            base = pl.multiple_of(lax.rem(i, per_rec) * s.chunk, s.chunk)
            out = jnp.zeros((s.chunk, lw), F32)
            for k in range(TAPS):
                out += taps_l[k] * ext_grad[r, l, pl.ds(base + dil_ref[k], s.chunk), :]
            gin_v[r, pl.ds(base, s.chunk), lanes] = out.astype(BF16)
            return 0

        lax.fori_loop(0, s.recs * per_rec, grad_step, 0, unroll=2)
    gin_copy = pltpu.make_async_copy(gin_v, gin_hbm, gin_sem)
    gin_copy.start()

    for o in range(1, s.nx):
        copy_sx(o, True).wait_recv()
    total = sx_v[0]
    for i in range(1, s.nx):
        total += sx_v[i]
    sz_v[z] = total
    for o in range(1, s.nz):
        copy_sz(o).start()

    out_stage2(0)
    in_stage3()

    for o in range(1, s.nz):
        copy_sz(o, True).wait_recv()
    total = sz_v[0]
    for i in range(1, s.nz):
        total += sz_v[i]
    sall_v[spot] = total
    for o in range(1, s.group):
        copy_sg(o).start()

    out_stage2(1)
    in_stage4()

    for o in range(1, s.group):
        copy_sg(o, True).wait_recv()

    def small_rows(which):
        return jnp.concatenate(
            [
                sall_v[2 * lane + which]
                for lane in range(d // s.sw)
            ],
            axis=1,
        )

    low, high = small_rows(0), small_rows(1)
    lam_g_re, lam_g_im, gain_g = high[2:3], high[3:4], high[4:5]
    radius_grad = lam_g_re * cos + lam_g_im * sin - gain_g * (radius / in_gain)
    packed_ref[0:8, :] = low * scale
    packed_ref[8:10, :] = high[0:2] * scale
    packed_ref[10:11, :] = -radius_grad * radius * decay_rate * scale
    packed_ref[11:12, :] = (lam_g_im * lam_re - lam_g_re * lam_im) * scale
    packed_ref[12:16, :] = jnp.zeros((4, d), F32)

    out_stage3()
    in_stage5()
    out_stage4()

    gin_copy.wait()
    for r in range(s.recs):
        act_halo(r).wait_send()
        grad_halo(r).wait_send()
    for way in range(2):
        for o in range(1, s.group):
            copy_a(way, o).wait_send()
        for o in range(1, s.nz):

            @pl.when(sends_b(way, o))
            def _():
                copy_b(way, o).wait_send()

    for w in range(2):
        for p in range(2):
            core_copy(w, p).wait_send()
    for o in range(1, s.group):
        copy_sr(o).wait_send()
        copy_sg(o).wait_send()
    for o in range(1, s.nx):
        in_copy1(o).wait_send()
        in_copy4(o).wait_send()
        out_copy3(o).wait_send()
        copy_sx(o).wait_send()
    for o in range(1, s.ny):
        in_copy2(o).wait_send()
        for p in range(2):
            out_copy1(p, o).wait_send()
    for o in range(1, s.nz):
        in_copy3(o).wait_send()
        copy_sz(o).wait_send()
    for i in range(s.nz):

        @pl.when(i != z)
        def _():
            out_copy2(i).wait_send()


def spread(gin_in, packed_ref, gin_out, taps_ref, skip_ref, rate_ref, angle_ref, win_ref, wout_ref):
    d = taps_ref.shape[1]
    gin_out[...] = gin_in[...]
    taps_ref[...] = packed_ref[0:TAPS, :]
    skip_ref[...] = packed_ref[9:10, :]
    rate_ref[...] = packed_ref[10:11, :]
    angle_ref[...] = packed_ref[11:12, :]
    win_ref[:, 0:d] = packed_ref[16:24, :]
    win_ref[:, d : 2 * d] = packed_ref[24:32, :]
    wout_ref[...] = packed_ref[32:48, :]


def on_device(
    lag,
    activations,
    cotangent,
    retain,
    dilation,
    conv_w,
    skip_gain,
    log_rate,
    mode_angle,
    w_in,
    w_out,
):
    recs, time_steps, features = activations.shape
    s = Sizes(lax.axis_size("tm"), lax.axis_size("rec"), time_steps, features, lag)
    d, t = s.d, s.t
    vmem = pl.BlockSpec(memory_space=pltpu.VMEM)
    smem = pl.BlockSpec(memory_space=pltpu.SMEM)
    hbm = pl.BlockSpec(memory_space=pl.ANY)
    pieces = s.nz * s.ny
    dma = pltpu.SemaphoreType.DMA
    buffers = [
        ((recs, t, d), BF16),
        ((recs, t, d), BF16),
        ((d, 2 * d), BF16),
        ((2 * d, d), BF16),
        ((recs, lag, d), BF16),
        ((recs, 4, t + lag, s.lw), F32),
        ((recs, 4, t + lag, s.lw), F32),
        ((recs, t, d), BF16),
        ((recs, t, d), BF16),
        ((recs, t, d), BF16),
        ((recs, t, s.lw), F32),
        ((recs, t, 2 * d), F32),
        ((recs, t, 2 * d), F32),
        ((recs, t, 2 * d), BF16),
        ((recs, t, 2 * d), BF16),
        ((recs, lag, d), BF16),
        ((recs, lag, d), BF16),
        ((recs, t, d), BF16),
        ((d, 2 * d), F32),
        ((2 * d, d), F32),
        ((2, s.group, 8, s.half + s.lw), F32),
        ((2, s.nz, 8, s.half + s.lw), F32),
        ((16, d), F32),
        ((8, d), F32),
        ((s.group, 8, s.sw), F32),
        ((s.group - 1, 8, s.sw), F32),
        ((s.nx, 8, s.sw), F32),
        ((s.nz, 8, s.sw), F32),
        ((s.group, 8, s.sw), F32),
        ((2, pieces, PIECE, d), BF16),
        ((2, pieces, PIECE, d), BF16),
        ((s.nx, s.ny, s.nz, PIECE, s.xw), BF16),
        ((s.nx - 1, s.ny, s.nz, PIECE, s.xw), BF16),
        ((s.ny, s.nz, PIECE, s.xw), BF16),
        ((s.ny - 1, s.nz, PIECE, s.xw), BF16),
        ((s.nz, PIECE, s.xw), BF16),
        ((s.nz - 1, PIECE, s.xw), BF16),
        ((s.nx, PIECE, s.xw), F32),
        ((s.ny, s.nz, PIECE, d), BF16),
        ((s.ny - 1, s.nz, PIECE, d), BF16),
        ((s.nz, PIECE, d), BF16),
        ((s.nz, PIECE, d), BF16),
        ((s.nx, PIECE, d), BF16),
    ]
    semaphores = [
        (4,),
        (recs, 2),
        (recs, 2),
        (),
        (2, s.group),
        (2, s.group),
        (2, s.nz),
        (2, s.nz),
        (2, 2, 2),
        (s.nx,),
        (s.nx,),
        (s.ny,),
        (s.ny,),
        (s.nz,),
        (s.nz,),
        (s.nx,),
        (s.nx,),
        (2, s.ny),
        (2, s.ny),
        (s.nz,),
        (s.nz,),
        (s.nx,),
        (s.nx,),
        (s.group,),
        (s.group,),
        (s.nx,),
        (s.nx,),
        (s.nz,),
        (s.nz,),
        (s.group,),
        (s.group,),
    ]
    gin, packed = pl.pallas_call(
        functools.partial(kernel, s),
        out_shape=(
            jax.ShapeDtypeStruct((recs, t, d), BF16),
            jax.ShapeDtypeStruct((48, d), F32),
        ),
        in_specs=[smem] + [vmem] * 5 + [hbm] * 4,
        out_specs=(hbm, vmem),
        scratch_shapes=[pltpu.VMEM(shape, dtype) for shape, dtype in buffers]
        + [dma if shape == () else dma(shape) for shape in semaphores],
        compiler_params=pltpu.CompilerParams(
            collective_id=0, has_side_effects=True, vmem_limit_bytes=56 * 1024 * 1024
        ),
        cost_estimate=pl.CostEstimate(
            flops=2 * 5 * recs * t * d * 2 * d, bytes_accessed=6 << 20, transcendentals=0
        ),
    )(
        dilation,
        retain,
        conv_w,
        skip_gain.reshape(1, d),
        log_rate.reshape(1, d),
        mode_angle.reshape(1, d),
        activations,
        cotangent,
        w_in,
        w_out,
    )
    grad_input, taps, skip, rate, angle, grad_w_in, grad_w_out = pl.pallas_call(
        spread,
        out_shape=(
            jax.ShapeDtypeStruct((recs, t, d), BF16),
            jax.ShapeDtypeStruct((TAPS, d), F32),
            jax.ShapeDtypeStruct((1, d), F32),
            jax.ShapeDtypeStruct((1, d), F32),
            jax.ShapeDtypeStruct((1, d), F32),
            jax.ShapeDtypeStruct((8, 2 * d), F32),
            jax.ShapeDtypeStruct((16, d), F32),
        ),
        in_specs=[vmem] * 2,
        out_specs=(vmem,) * 7,
    )(gin, packed)
    return (
        grad_input,
        taps,
        skip.reshape(d),
        rate.reshape(d),
        angle.reshape(d),
        grad_w_in,
        grad_w_out,
    )


def build(mesh, lag):
    wide = P("rec", "tm", None)
    return jax.shard_map(
        functools.partial(on_device, lag),
        mesh=mesh,
        in_specs=(wide, wide, P("rec", "tm")) + (P(),) * 7,
        out_specs=(wide, P(), P(), P(), P(), P("tm", None), P("tm", None)),
        check_vma=False,
    )


def solution(mesh):
    return build(mesh, MAXLAG)
```

```python
import functools
import math

import jax
import jax.numpy as jnp
from jax import lax
from jax.experimental import pallas as pl
from jax.experimental.pallas import tpu as pltpu
from jax.sharding import PartitionSpec as P

TAPS = 9
MAXLAG = 128
NB = 8
PIECE = 16
F32 = jnp.float32
BF16 = jnp.bfloat16


class Sizes:
    def __init__(self, tm, rec, time_steps, features, lag):
        self.core = 2
        self.nx = rec
        self.ny = 4 if tm >= 64 else 2
        self.nz = tm // (self.core * self.ny)
        self.group = self.core * self.ny
        self.recs = 2
        self.t = time_steps
        self.d = features
        self.lag = lag
        self.bl = time_steps // NB
        self.lw = features // 4
        self.half = features // 2
        self.xw = features // rec
        self.sw = 2 * features // self.nz
        self.chunk = min(64, lag)
        self.hz = self.nz // 2


def mul(ar, ai, br, bi):
    return ar * br - ai * bi, ar * bi + ai * br


def square_times(re, im, times):
    for _ in range(times):
        re, im = re * re - im * im, 2.0 * (re * im)
    return re, im


def one_minus_exp(u):
    series = jnp.ones_like(u)
    for n in range(12, 1, -1):
        series = 1.0 - u * (1.0 / n) * series
    return jnp.where(u < 1.0, u * series, 1.0 - jnp.exp(-u))


def log2(n):
    return n.bit_length() - 1


def kernel(
    s,
    dil_ref,
    retain_hbm,
    convw_hbm,
    skip_hbm,
    rate_hbm,
    angle_hbm,
    act_hbm,
    cot_hbm,
    win_hbm,
    wout_hbm,
    gin_hbm,
    packed_ref,
    retain_ref,
    convw_ref,
    skip_ref,
    rate_ref,
    angle_ref,
    act_v,
    cot_v,
    win_v,
    wout_v,
    halo_v,
    ext_act,
    ext_grad,
    cotp_v,
    convb_v,
    convp_v,
    keep_v,
    e_v,
    x_v,
    hb_v,
    gx_v,
    head_v,
    ghalo_v,
    gin_v,
    gx_time_v,
    scan_a,
    scan_b,
    small_v,
    skip_v,
    ssend,
    srecv,
    sx_v,
    sp_v,
    sall_v,
    piece_v,
    recv_w,
    in_chip,
    in_recv1,
    in_sum1,
    in_recv2,
    in_sum2,
    in_recv3,
    in_full,
    out_chip,
    out_recv1,
    out_sum1,
    out_recv2,
    out_x,
    in_sem,
    halo_sem,
    ghalo_sem,
    gin_sem,
    a_send,
    a_recv,
    b_send,
    b_recv,
    wc_sem,
    i1_send,
    i1_recv,
    i2_send,
    i2_recv,
    i3_send,
    i3_recv,
    i4_send,
    i4_recv,
    o1_send,
    o1_recv,
    o2_send,
    o2_recv,
    o3_send,
    o3_recv,
    sr_send,
    sr_recv,
    sx_send,
    sx_recv,
    sp_send,
    sp_recv,
    sg_send,
    sg_recv,
):
    t_len, d, half, lw = s.t, s.d, s.half, s.lw
    tm = lax.axis_index("tm")
    rec = lax.axis_index("rec")
    core = lax.rem(tm, s.core)
    y = lax.rem(tm // s.core, s.ny)
    z = tm // s.group
    spot = lax.rem(tm, s.group)
    tm_count = s.nz * s.group
    other = 1 - core

    def at(tm_to, rec_to):
        return (tm_to, rec_to)

    def at_group(o):
        return at(z * s.group + lax.rem(spot + o, s.group), rec)

    def at_core():
        return at(tm + 1 - 2 * core, rec)

    def at_y(o):
        return at(z * s.group + lax.rem(y + o, s.ny) * s.core + core, rec)

    def at_z(o):
        return at(lax.rem(z + o, s.nz) * s.group + spot, rec)

    def at_x(o):
        return at(tm, lax.rem(rec + o, s.nx))

    def at_tm(o):
        return at(lax.rem(tm + o + tm_count, tm_count), rec)

    def remote(src, dst, ssem, rsem, to):
        return pltpu.make_async_remote_copy(
            src_ref=src,
            dst_ref=dst,
            send_sem=ssem,
            recv_sem=rsem,
            device_id=to,
            device_id_type=pl.DeviceIdType.MESH,
        )

    loads = [
        pltpu.make_async_copy(src, dst, in_sem.at[i])
        for i, (src, dst) in enumerate(
            (
                (retain_hbm, retain_ref),
                (rate_hbm, rate_ref),
                (angle_hbm, angle_ref),
                (cot_hbm, cot_v),
                (wout_hbm, wout_v),
                (act_hbm, act_v),
                (convw_hbm, convw_ref),
                (win_hbm, win_v),
                (skip_hbm, skip_ref),
            )
        )
    ]
    barrier = pltpu.get_barrier_semaphore()
    partners = (
        [at_group(o) for o in range(1, s.group)]
        + [at_z(o) for o in range(1, s.nz)]
        + [at_x(o) for o in range(1, s.nx)]
        + [at_tm(1), at_tm(-1)]
    )
    for partner in partners:
        pl.semaphore_signal(
            barrier, inc=1, device_id=partner, device_id_type=pl.DeviceIdType.MESH
        )
    for load in loads:
        load.start()
    pl.semaphore_wait(barrier, len(partners))

    def act_halo(r):
        return remote(
            act_hbm.at[r, pl.ds(t_len - s.lag, s.lag), :],
            halo_v.at[r],
            halo_sem.at[r, 0],
            halo_sem.at[r, 1],
            at_tm(1),
        )

    for r in range(s.recs):
        act_halo(r).start()

    row = lax.broadcasted_iota(jnp.int32, (t_len, t_len), 0)
    col = lax.broadcasted_iota(jnp.int32, (t_len, t_len), 1)
    chosen = col == lax.rem(row, NB) * s.bl + row // NB
    order = jnp.where(chosen, 1.0, 0.0).astype(BF16)
    chosen_back = row == lax.rem(col, NB) * s.bl + col // NB
    order_back = jnp.where(chosen_back, 1.0, 0.0).astype(BF16)
    all_rows = s.recs * t_len
    for i in range(3):
        loads[i].wait()
    for r in range(s.recs):
        picked = jnp.sum(
            jnp.where(chosen, retain_ref[r : r + 1, :], 0.0), axis=1, keepdims=True
        )
        keep_v[r] = jnp.broadcast_to(picked, (t_len, lw))

    decay_rate = jnp.exp(rate_ref[...])
    radius = jnp.exp(-decay_rate)
    cos, sin = jnp.cos(angle_ref[...]), jnp.sin(angle_ref[...])
    lam_re = radius * cos
    lam_im = radius * sin
    in_gain = jnp.sqrt(one_minus_exp(2.0 * decay_rate))
    block_pow = [square_times(lam_re, lam_im, log2(s.bl))]
    for _ in range(2):
        block_pow.append(square_times(*block_pow[-1], 1))
    dev_pow = square_times(*block_pow[-1], 1)
    plane_pow = square_times(*dev_pow, log2(s.group))

    def packed(v):
        pair = jnp.concatenate([v[:, :half], v[:, half:]], axis=0)
        return jnp.concatenate([pair] * s.recs, axis=0)

    dev_pack = (packed(dev_pow[0]), packed(dev_pow[1]))
    plane_pack = (packed(plane_pow[0]), packed(plane_pow[1]))
    sub_row = lax.broadcasted_iota(jnp.int32, (NB, d), 0)
    sub_row_k = lax.broadcasted_iota(jnp.int32, (NB, lw), 0)

    def power_table(index):
        re = jnp.ones((NB, d), F32)
        im = jnp.zeros((NB, d), F32)
        for bit, (pr, pi) in zip((1, 2, 4), block_pow):
            nr, ni = mul(re, im, pr, pi)
            here = lax.rem(index // bit, 2) == 1
            re = jnp.where(here, nr, re)
            im = jnp.where(here, ni, im)
        return re, im

    def wide(k):
        return jnp.concatenate([k] * (d // k.shape[1]), axis=1)

    def block_scan(e_re, e_im, k, sign):
        for span, (pr, pi) in zip((1, 2, 4), block_pow):
            shift = span if sign > 0 else NB - span
            pi = sign * pi
            n_re = pltpu.roll(e_re, shift, 0)
            n_im = pltpu.roll(e_im, shift, 0)
            n_k = pltpu.roll(k, shift, 0)
            there = sub_row >= span if sign > 0 else sub_row < NB - span
            there_k = sub_row_k >= span if sign > 0 else sub_row_k < NB - span
            m_re, m_im = mul(pr, pi, n_re, n_im)
            k_wide = wide(k)
            e_re = e_re + jnp.where(there, k_wide * m_re, 0.0)
            e_im = e_im + jnp.where(there, k_wide * m_im, 0.0)
            k = jnp.where(there_k, k * n_k, k)
        return e_re, e_im, k

    def summarize(way, scans):
        last = NB - 1 if way == 0 else 0
        for r in range(s.recs):
            e_re, e_im, k = scans[r]
            for part, v in enumerate((e_re, e_im)):
                for h in range(2):
                    at_row = part * 4 + r * 2 + h
                    scan_a[way, spot, at_row : at_row + 1, 0:half] = v[
                        last : last + 1, h * half : (h + 1) * half
                    ]
                    scan_a[way, spot, at_row : at_row + 1, half : half + lw] = k[
                        last : last + 1, :
                    ]

    def copy_a(way, o, back=False):
        held = scan_a.at[way, lax.rem(spot + s.group - o, s.group) if back else spot]
        return remote(held, held, a_send.at[way, o], a_recv.at[way, o], at_group(o))

    def copy_b(way, o, back=False):
        held = scan_b.at[way, lax.rem(z + s.nz - o, s.nz) if back else z]
        return remote(held, held, b_send.at[way, o], b_recv.at[way, o], at_z(o))

    def sends_b(way, o):
        return z + o < s.nz if way == 0 else z + o >= s.nz

    def gets_b(way, o):
        return z - o >= 0 if way == 0 else z - o < 0

    def start_a(way):
        for o in range(1, s.group):
            copy_a(way, o).start()

    def advance(slot, state, pack, way):
        sign = 1.0 if way == 0 else -1.0
        k = slot[0:4, half : half + lw]
        k = jnp.concatenate([k] * (half // lw), axis=1)
        m_re, m_im = mul(pack[0], sign * pack[1], state[0], state[1])
        return slot[0:4, 0:half] + k * m_re, slot[4:8, 0:half] + k * m_im

    def in_order(count, way):
        return range(count) if way == 0 else range(count - 1, -1, -1)

    def plane_step(way):
        for o in range(1, s.group):
            copy_a(way, o, True).wait_recv()
        state = (jnp.zeros((4, half), F32), jnp.zeros((4, half), F32))
        k_all = jnp.ones((4, lw), F32)
        for i in in_order(s.group, way):
            slot = scan_a[way, i]
            state = advance(slot, state, dev_pack, way)
            k_all = k_all * slot[0:4, half : half + lw]
        scan_b[way, z, 0:4, 0:half] = state[0]
        scan_b[way, z, 4:8, 0:half] = state[1]
        scan_b[way, z, 0:4, half : half + lw] = k_all
        scan_b[way, z, 4:8, half : half + lw] = k_all
        for o in range(1, s.nz):

            @pl.when(sends_b(way, o))
            def _():
                copy_b(way, o).start()

    def entering(way):
        for o in range(1, s.nz):

            @pl.when(gets_b(way, o))
            def _():
                copy_b(way, o, True).wait_recv()

        state = (jnp.zeros((4, half), F32), jnp.zeros((4, half), F32))
        for i in in_order(s.nz, way):
            moved = advance(scan_b[way, i], state, plane_pack, way)
            use = i < z if way == 0 else i > z
            state = tuple(jnp.where(use, m, o) for m, o in zip(moved, state))
        for i in in_order(s.group, way):
            moved = advance(scan_a[way, i], state, dev_pack, way)
            use = i < spot if way == 0 else i > spot
            state = tuple(jnp.where(use, m, o) for m, o in zip(moved, state))
        return state

    def block_entry(way, scans, state):
        sign = 1.0 if way == 0 else -1.0
        index = sub_row if way == 0 else NB - 1 - sub_row
        pw_re, pw_im = power_table(index)
        pw_im = sign * pw_im
        shift = 1 if way == 0 else NB - 1
        out = []
        for r in range(s.recs):
            s_re, s_im = (
                jnp.concatenate([v[2 * r : 2 * r + 1], v[2 * r + 1 : 2 * r + 2]], axis=1)
                for v in state
            )
            e_re, e_im, k = scans[r]
            m_re, m_im = mul(pw_re, pw_im, s_re, s_im)
            k_wide = wide(pltpu.roll(k, shift, 0))
            first = index == 0
            out.append(
                (
                    jnp.where(first, s_re, pltpu.roll(e_re, shift, 0) + k_wide * m_re),
                    jnp.where(first, s_im, pltpu.roll(e_im, shift, 0) + k_wide * m_im),
                )
            )
        return out

    lr = jnp.broadcast_to(lam_re, (NB, d))
    li = jnp.broadcast_to(lam_im, (NB, d))
    gain = jnp.broadcast_to(in_gain, (NB, d))
    zero = jnp.zeros((NB, d), F32)

    def rows(j):
        return pl.ds(pl.multiple_of(j * NB, NB), NB)

    def rows2(i):
        return pl.ds(pl.multiple_of(i * 2 * NB, 2 * NB), 2 * NB)

    loads[3].wait()
    loads[4].wait()
    nt = (((1,), (1,)), ((), ()))
    tn = (((0,), (0,)), ((), ()))
    for r in range(s.recs):
        cotp_v[r] = jnp.dot(order, cot_v[r], preferred_element_type=F32).astype(BF16)
    cot_rows = cotp_v[...].reshape(all_rows, d)
    back = lax.dot_general(cot_rows, wout_v[...], nt, preferred_element_type=F32)
    e_v[...] = back.reshape(s.recs, t_len, 2 * d)

    def adj_first(i, carry):
        j = s.bl - 1 - i
        new = []
        for r in range(s.recs):
            p_re, p_im, k_all = carry[r]
            k = keep_v[r, rows(j), :]
            k4 = wide(k)
            d_re = e_v[r, rows(j), 0:d] + p_re
            d_im = e_v[r, rows(j), d : 2 * d] + p_im
            m_re, m_im = mul(lr, -li, d_re, d_im)
            new.append((k4 * m_re, k4 * m_im, k_all * k))
        return tuple(new)

    ones_k = jnp.ones((NB, lw), F32)
    ends = lax.fori_loop(0, s.bl, adj_first, ((zero, zero, ones_k),) * s.recs, unroll=4)
    keeps = [ends[r][2] for r in range(s.recs)]
    adj_scans = [block_scan(*ends[r], -1.0) for r in range(s.recs)]
    summarize(1, adj_scans)
    start_a(1)

    loads[5].wait()
    loads[6].wait()
    for r in range(s.recs):
        for l in range(4):
            ext_act[r, l, s.lag : s.lag + t_len, :] = act_v[
                r, :, l * lw : (l + 1) * lw
            ].astype(F32)
    per_rec = t_len // s.chunk

    def fold(v):
        return jnp.sum(v.reshape(s.chunk // 8, 8, lw), axis=0)

    def conv_block(l, r, base):
        lanes = slice(l * lw, (l + 1) * lw)
        base = pl.multiple_of(base, s.chunk)
        out = jnp.zeros((s.chunk, lw), F32)
        for k in range(TAPS):
            shifted = ext_act[r, l, pl.ds(base + s.lag - dil_ref[k], s.chunk), :]
            out += convw_ref[k : k + 1, lanes] * shifted
        convb_v[r, pl.ds(base, s.chunk), lanes] = out.astype(BF16)
        return fold(out * cot_v[r, pl.ds(base, s.chunk), lanes].astype(F32))

    low_chunks = s.lag // s.chunk
    high_chunks = per_rec - low_chunks
    none = jnp.zeros((8, lw), F32)
    for l in range(4):

        def high_step(i, acc):
            base = s.lag + lax.rem(i, high_chunks) * s.chunk
            return acc + conv_block(l, i // high_chunks, base)

        acc = lax.fori_loop(0, s.recs * high_chunks, high_step, none, unroll=2)
        skip_v[:, l * lw : (l + 1) * lw] = acc

    plane_step(1)

    loads[7].wait()
    loads[8].wait()
    for r in range(s.recs):
        act_halo(r).wait_recv()
        for l in range(4):
            lanes = slice(l * lw, (l + 1) * lw)
            before = halo_v[r, :, lanes].astype(F32)
            ext_act[r, l, 0 : s.lag, :] = jnp.where(tm > 0, before, 0.0)

            def low_step(i, acc):
                return acc + conv_block(l, r, i * s.chunk)

            skip_v[:, lanes] += lax.fori_loop(0, low_chunks, low_step, none, unroll=2)
        convp_v[r] = jnp.dot(order, convb_v[r], preferred_element_type=F32).astype(BF16)
    conv_rows = convp_v[...].reshape(all_rows, d)
    x_v[...] = jnp.dot(conv_rows, win_v[...], preferred_element_type=F32).reshape(
        s.recs, t_len, 2 * d
    )

    def fwd_first(j, carry):
        new = []
        for r in range(s.recs):
            h_re, h_im = carry[r]
            k4 = wide(keep_v[r, rows(j), :])
            m_re, m_im = mul(lr, li, h_re, h_im)
            new.append(
                (
                    k4 * m_re + x_v[r, rows(j), 0:d],
                    k4 * m_im + x_v[r, rows(j), d : 2 * d],
                )
            )
        return tuple(new)

    ends = lax.fori_loop(0, s.bl, fwd_first, ((zero, zero),) * s.recs, unroll=4)
    fwd_scans = [block_scan(*ends[r], keeps[r], 1.0) for r in range(s.recs)]
    summarize(0, fwd_scans)
    start_a(0)

    entry = block_entry(1, adj_scans, entering(1))

    def adj_second(i, carry):
        i = s.bl // 2 - 1 - i
        new = []
        for r in range(s.recs):
            p_re, p_im = carry[r]
            held = [None, None]
            for sub in (1, 0):
                j = 2 * i + sub
                k4 = wide(keep_v[r, rows(j), :])
                d_re = e_v[r, rows(j), 0:d] + p_re
                d_im = e_v[r, rows(j), d : 2 * d] + p_im
                e_v[r, rows(j), 0:d] = d_re
                e_v[r, rows(j), d : 2 * d] = d_im
                held[sub] = (gain * d_re, gain * d_im)
                m_re, m_im = mul(lr, -li, d_re, d_im)
                p_re, p_im = k4 * m_re, k4 * m_im
            for part in range(2):
                gx_v[r, rows2(i), part * d : (part + 1) * d] = jnp.concatenate(
                    [held[0][part], held[1][part]], axis=0
                ).astype(BF16)
            new.append((p_re, p_im))
        return tuple(new)

    lax.fori_loop(0, s.bl // 2, adj_second, tuple(entry), unroll=2)

    pieces = s.nz * s.ny
    part = pieces // 2

    def core_copy(w, p):
        some = pl.ds(p * part, part)
        return remote(
            piece_v.at[w, some, other],
            recv_w.at[w, some],
            wc_sem.at[w, p, 0],
            wc_sem.at[w, p, 1],
            at_core(),
        )

    def chip_sum(w, g):
        return (piece_v[w, g, core].astype(F32) + recv_w[w, g].astype(F32)).astype(BF16)

    def in_copy1(o):
        src = in_chip.at[lax.rem(rec + o, s.nx)]
        return remote(src, in_recv1.at[o - 1], i1_send.at[o], i1_recv.at[o], at_x(o))

    def in_copy2(o):
        src = in_sum1.at[lax.rem(z + o, s.nz)]
        return remote(src, in_recv2.at[o - 1], i2_send.at[o], i2_recv.at[o], at_z(o))

    def in_copy3(o):
        src = in_sum2.at[lax.rem(y + o, s.ny)]
        return remote(src, in_recv3.at[o - 1], i3_send.at[o], i3_recv.at[o], at_y(o))

    def in_copy4(o, back=False):
        held = in_full.at[lax.rem(rec + s.nx - o, s.nx) if back else rec]
        return remote(held, held, i4_send.at[o], i4_recv.at[o], at_x(o))

    def in_stage1():
        for p in range(2):
            core_copy(0, p).wait_recv()

        def one(g, _):
            total = chip_sum(0, g)
            for i in range(s.nx):
                in_chip[i, g // s.ny, lax.rem(g, s.ny)] = total[:, i * s.xw : (i + 1) * s.xw]
            return 0

        lax.fori_loop(0, pieces, one, 0, unroll=4)
        for o in range(1, s.nx):
            in_copy1(o).start()

    def in_stage2():
        for o in range(1, s.nx):
            in_copy1(o).wait_recv()

        def one(i, _):
            total = in_chip[rec, i].astype(F32)
            for o in range(1, s.nx):
                total += in_recv1[o - 1, i].astype(F32)
            in_sum1[i] = total.astype(BF16)
            return 0

        lax.fori_loop(0, s.nz, one, 0, unroll=2)
        for o in range(1, s.nz):
            in_copy2(o).start()

    def in_stage3():
        for o in range(1, s.nz):
            in_copy2(o).wait_recv()
        total = in_sum1[z].astype(F32)
        for o in range(1, s.nz):
            total += in_recv2[o - 1].astype(F32)
        in_sum2[...] = total.astype(BF16)
        for o in range(1, s.ny):
            in_copy3(o).start()

    scale = 1.0 / math.sqrt(s.recs * s.nx * t_len * tm_count)

    def in_stage4():
        for o in range(1, s.ny):
            in_copy3(o).wait_recv()
        total = in_sum2[y].astype(F32)
        for o in range(1, s.ny):
            total += in_recv3[o - 1].astype(F32)
        in_full[rec] = total * scale
        for o in range(1, s.nx):
            in_copy4(o).start()

    def in_stage5():
        for o in range(1, s.nx):
            in_copy4(o, True).wait_recv()
        block = jnp.concatenate([in_full[i] for i in range(s.nx)], axis=1)
        packed_ref[16:32, :] = block

    def out_copy1(p, o):
        some = pl.ds(p * s.hz, s.hz)
        return remote(
            out_chip.at[lax.rem(y + o, s.ny), some],
            out_recv1.at[o - 1, some],
            o1_send.at[p, o],
            o1_recv.at[p, o],
            at_y(o),
        )

    def out_copy2(to):
        return remote(
            out_sum1.at[to],
            out_recv2.at[z],
            o2_send.at[to],
            o2_recv.at[z],
            at(to * s.group + spot, rec),
        )

    def out_from2(z_from):
        held = out_recv2.at[z_from]
        return remote(
            held, held, o2_send.at[z_from], o2_recv.at[z_from], at(z_from * s.group + spot, rec)
        )

    def out_copy3(o, back=False):
        held = out_x.at[lax.rem(rec + s.nx - o, s.nx) if back else rec]
        return remote(held, held, o3_send.at[o], o3_recv.at[o], at_x(o))

    def out_stage1(p):
        core_copy(1, p).wait_recv()

        def one(g, _):
            out_chip[lax.rem(g, s.ny), g // s.ny] = chip_sum(1, g)
            return 0

        lax.fori_loop(p * part, (p + 1) * part, one, 0, unroll=2)
        for o in range(1, s.ny):
            out_copy1(p, o).start()

    def out_stage2(p):
        for o in range(1, s.ny):
            out_copy1(p, o).wait_recv()
        for i in range(p * s.hz, (p + 1) * s.hz):
            total = out_chip[y, i].astype(F32)
            for o in range(1, s.ny):
                total += out_recv1[o - 1, i].astype(F32)
            out_sum1[i] = total.astype(BF16)

            @pl.when(i != z)
            def _():
                out_copy2(i).start()

    def out_stage3():
        for i in range(s.nz):

            @pl.when(i != z)
            def _():
                out_from2(i).wait_recv()

        out_recv2[z] = out_sum1[z]
        total = out_recv2[0].astype(F32)
        for i in range(1, s.nz):
            total += out_recv2[i].astype(F32)
        out_x[rec] = total.astype(BF16)
        for o in range(1, s.nx):
            out_copy3(o).start()

    def out_stage4():
        for o in range(1, s.nx):
            out_copy3(o, True).wait_recv()
        total = out_x[0].astype(F32)
        for i in range(1, s.nx):
            total += out_x[i].astype(F32)
        packed_ref[32:48, :] = total * scale

    half_d = d // 2
    for p in range(2):
        total = lax.dot_general(
            convp_v[:, :, p * half_d : (p + 1) * half_d].reshape(all_rows, half_d),
            gx_v[...].reshape(all_rows, 2 * d),
            tn,
            preferred_element_type=F32,
        ).reshape(part, s.core, 8, 2 * d)
        total = jnp.concatenate([total[..., 0:d], total[..., d : 2 * d]], axis=2)
        piece_v[0, p * part : (p + 1) * part] = total.astype(BF16)
        core_copy(0, p).start()

    plane_step(0)

    def grad_halo(r):
        return remote(
            head_v.at[r], ghalo_v.at[r], ghalo_sem.at[r, 0], ghalo_sem.at[r, 1], at_tm(-1)
        )

    for r in range(s.recs):
        gx_time_v[r] = jnp.dot(order_back, gx_v[r], preferred_element_type=F32).astype(BF16)
    gx_rows = gx_time_v[...].reshape(all_rows, 2 * d)
    grads = lax.dot_general(gx_rows, win_v[...], nt, preferred_element_type=F32)
    for r in range(s.recs):
        grad = grads[r * t_len : (r + 1) * t_len]
        grad += skip_ref[...] * cot_v[r].astype(F32)
        head_v[r] = grad[0 : s.lag, :].astype(BF16)
        for l in range(4):
            ext_grad[r, l, 0:t_len, :] = grad[:, l * lw : (l + 1) * lw]
        grad_halo(r).start()

    in_stage1()

    for l in range(4):
        lanes = slice(l * lw, (l + 1) * lw)

        def tap_step(i, acc):
            r = i // per_rec
            base = pl.multiple_of(lax.rem(i, per_rec) * s.chunk, s.chunk)
            grad = ext_grad[r, l, pl.ds(base, s.chunk), :]
            return tuple(
                acc[k]
                + fold(grad * ext_act[r, l, pl.ds(base + s.lag - dil_ref[k], s.chunk), :])
                for k in range(TAPS)
            )

        acc = lax.fori_loop(0, s.recs * per_rec, tap_step, (none,) * TAPS, unroll=2)
        for k in range(TAPS):
            small_v[k : k + 1, lanes] = jnp.sum(acc[k], axis=0, keepdims=True)
    small_v[9:10, :] = jnp.sum(skip_v[...], axis=0, keepdims=True)

    entry = block_entry(0, fwd_scans, entering(0))

    def fwd_second(i, carry):
        state, sums = carry
        new = []
        s_re, s_im, s_gain = sums
        for r in range(s.recs):
            h_re, h_im = state[r]
            held = [None, None]
            for sub in (0, 1):
                j = 2 * i + sub
                k4 = wide(keep_v[r, rows(j), :])
                kh_re, kh_im = k4 * h_re, k4 * h_im
                d_re = e_v[r, rows(j), 0:d]
                d_im = e_v[r, rows(j), d : 2 * d]
                x_re = x_v[r, rows(j), 0:d]
                x_im = x_v[r, rows(j), d : 2 * d]
                s_re += d_re * kh_re + d_im * kh_im
                s_im += d_im * kh_re - d_re * kh_im
                s_gain += d_re * x_re + d_im * x_im
                m_re, m_im = mul(lr, li, kh_re, kh_im)
                h_re = m_re + x_re
                h_im = m_im + x_im
                held[sub] = (gain * h_re, gain * h_im)
            for part in range(2):
                hb_v[r, rows2(i), part * d : (part + 1) * d] = jnp.concatenate(
                    [held[0][part], held[1][part]], axis=0
                ).astype(BF16)
            new.append((h_re, h_im))
        return tuple(new), (s_re, s_im, s_gain)

    _, sums = lax.fori_loop(
        0, s.bl // 2, fwd_second, (tuple(entry), (zero, zero, zero)), unroll=2
    )
    for p in range(2):
        total = lax.dot_general(
            hb_v[:, :, p * d : (p + 1) * d].reshape(all_rows, d),
            cotp_v[...].reshape(all_rows, d),
            tn,
            preferred_element_type=F32,
        )
        piece_v[1, p * part : (p + 1) * part] = total.astype(BF16).reshape(
            part, s.core, PIECE, d
        )
        core_copy(1, p).start()

    out_stage1(0)
    out_stage1(1)

    sums = (in_gain * sums[0], in_gain * sums[1], sums[2])
    for i, v in enumerate(sums):
        small_v[10 + i : 11 + i, :] = jnp.sum(v, axis=0, keepdims=True)
    small_v[13:16, :] = jnp.zeros((3, d), F32)

    for i in range(s.nz):
        lane = (i // 2) * s.sw
        ssend[i] = small_v[(i % 2) * 8 : (i % 2) * 8 + 8, lane : lane + s.sw]

    def copy_sr(o):
        src = ssend.at[lax.rem(z + o, s.nz)]
        return remote(src, srecv.at[o - 1], sr_send.at[o], sr_recv.at[o], at_z(o))

    def copy_sx(o, back=False):
        held = sx_v.at[lax.rem(rec + s.nx - o, s.nx) if back else rec]
        return remote(held, held, sx_send.at[o], sx_recv.at[o], at_x(o))

    def copy_sp(o, back=False):
        held = sp_v.at[lax.rem(spot + s.group - o, s.group) if back else spot]
        return remote(held, held, sp_send.at[o], sp_recv.at[o], at_group(o))

    def copy_sg(o, back=False):
        held = sall_v.at[lax.rem(z + s.nz - o, s.nz) if back else z]
        return remote(held, held, sg_send.at[o], sg_recv.at[o], at_z(o))

    for o in range(1, s.nz):
        copy_sr(o).start()

    in_stage2()

    for r in range(s.recs):
        grad_halo(r).wait_recv()
        for l in range(4):
            after = ghalo_v[r, :, l * lw : (l + 1) * lw].astype(F32)
            ext_grad[r, l, t_len : t_len + s.lag, :] = jnp.where(tm < tm_count - 1, after, 0.0)
    for l in range(4):
        lanes = slice(l * lw, (l + 1) * lw)
        taps_l = [convw_ref[k : k + 1, lanes] for k in range(TAPS)]

        def grad_step(i, _):
            r = i // per_rec
            base = pl.multiple_of(lax.rem(i, per_rec) * s.chunk, s.chunk)
            out = jnp.zeros((s.chunk, lw), F32)
            for k in range(TAPS):
                out += taps_l[k] * ext_grad[r, l, pl.ds(base + dil_ref[k], s.chunk), :]
            gin_v[r, pl.ds(base, s.chunk), lanes] = out.astype(BF16)
            return 0

        lax.fori_loop(0, s.recs * per_rec, grad_step, 0, unroll=2)
    gin_copy = pltpu.make_async_copy(gin_v, gin_hbm, gin_sem)
    gin_copy.start()

    for o in range(1, s.nz):
        copy_sr(o).wait_recv()
    total = ssend[z]
    for o in range(1, s.nz):
        total += srecv[o - 1]
    sx_v[rec] = total
    for o in range(1, s.nx):
        copy_sx(o).start()

    out_stage2(0)

    for o in range(1, s.nx):
        copy_sx(o, True).wait_recv()
    total = sx_v[0]
    for i in range(1, s.nx):
        total += sx_v[i]
    sp_v[spot] = total
    for o in range(1, s.group):
        copy_sp(o).start()

    out_stage2(1)

    in_stage3()

    for o in range(1, s.group):
        copy_sp(o, True).wait_recv()
    total = sp_v[0]
    for i in range(1, s.group):
        total += sp_v[i]
    sall_v[z] = total
    for o in range(1, s.nz):
        copy_sg(o).start()

    out_stage3()
    in_stage4()

    for o in range(1, s.nz):
        copy_sg(o, True).wait_recv()

    def small_rows(which):
        return jnp.concatenate(
            [
                sall_v[2 * lane + which]
                for lane in range(d // s.sw)
            ],
            axis=1,
        )

    low, high = small_rows(0), small_rows(1)
    lam_g_re, lam_g_im, gain_g = high[2:3], high[3:4], high[4:5]
    radius_grad = lam_g_re * cos + lam_g_im * sin - gain_g * (radius / in_gain)
    packed_ref[0:8, :] = low * scale
    packed_ref[8:10, :] = high[0:2] * scale
    packed_ref[10:11, :] = -radius_grad * radius * decay_rate * scale
    packed_ref[11:12, :] = (lam_g_im * lam_re - lam_g_re * lam_im) * scale
    packed_ref[12:16, :] = jnp.zeros((4, d), F32)

    for r in range(s.recs):
        act_halo(r).wait_send()
        grad_halo(r).wait_send()
    for way in range(2):
        for o in range(1, s.group):
            copy_a(way, o).wait_send()
        for o in range(1, s.nz):

            @pl.when(sends_b(way, o))
            def _():
                copy_b(way, o).wait_send()

    for w in range(2):
        for p in range(2):
            core_copy(w, p).wait_send()
    for o in range(1, s.group):
        copy_sp(o).wait_send()
    for o in range(1, s.nx):
        in_copy1(o).wait_send()
        copy_sx(o).wait_send()
    for o in range(1, s.ny):
        for p in range(2):
            out_copy1(p, o).wait_send()
    for o in range(1, s.nz):
        in_copy2(o).wait_send()
        copy_sr(o).wait_send()

    in_stage5()
    out_stage4()

    gin_copy.wait()
    for o in range(1, s.nz):
        copy_sg(o).wait_send()
    for o in range(1, s.nx):
        in_copy4(o).wait_send()
        out_copy3(o).wait_send()
    for o in range(1, s.ny):
        in_copy3(o).wait_send()
    for i in range(s.nz):

        @pl.when(i != z)
        def _():
            out_copy2(i).wait_send()


def spread(gin_in, packed_ref, gin_out, taps_ref, skip_ref, rate_ref, angle_ref, win_ref, wout_ref):
    d = taps_ref.shape[1]
    gin_out[...] = gin_in[...]
    taps_ref[...] = packed_ref[0:TAPS, :]
    skip_ref[...] = packed_ref[9:10, :]
    rate_ref[...] = packed_ref[10:11, :]
    angle_ref[...] = packed_ref[11:12, :]
    win_ref[:, 0:d] = packed_ref[16:24, :]
    win_ref[:, d : 2 * d] = packed_ref[24:32, :]
    wout_ref[...] = packed_ref[32:48, :]


def on_device(
    lag,
    activations,
    cotangent,
    retain,
    dilation,
    conv_w,
    skip_gain,
    log_rate,
    mode_angle,
    w_in,
    w_out,
):
    recs, time_steps, features = activations.shape
    s = Sizes(lax.axis_size("tm"), lax.axis_size("rec"), time_steps, features, lag)
    d, t = s.d, s.t
    vmem = pl.BlockSpec(memory_space=pltpu.VMEM)
    smem = pl.BlockSpec(memory_space=pltpu.SMEM)
    hbm = pl.BlockSpec(memory_space=pl.ANY)
    pieces = s.nz * s.ny
    dma = pltpu.SemaphoreType.DMA
    buffers = [
        ((recs, t), F32),
        ((TAPS, d), F32),
        ((1, d), F32),
        ((1, d), F32),
        ((1, d), F32),
        ((recs, t, d), BF16),
        ((recs, t, d), BF16),
        ((d, 2 * d), BF16),
        ((2 * d, d), BF16),
        ((recs, lag, d), BF16),
        ((recs, 4, t + lag, s.lw), F32),
        ((recs, 4, t + lag, s.lw), F32),
        ((recs, t, d), BF16),
        ((recs, t, d), BF16),
        ((recs, t, d), BF16),
        ((recs, t, s.lw), F32),
        ((recs, t, 2 * d), F32),
        ((recs, t, 2 * d), F32),
        ((recs, t, 2 * d), BF16),
        ((recs, t, 2 * d), BF16),
        ((recs, lag, d), BF16),
        ((recs, lag, d), BF16),
        ((recs, t, d), BF16),
        ((recs, t, 2 * d), BF16),
        ((2, s.group, 8, s.half + s.lw), F32),
        ((2, s.nz, 8, s.half + s.lw), F32),
        ((16, d), F32),
        ((8, d), F32),
        ((s.nz, 8, s.sw), F32),
        ((s.nz - 1, 8, s.sw), F32),
        ((s.nx, 8, s.sw), F32),
        ((s.group, 8, s.sw), F32),
        ((s.nz, 8, s.sw), F32),
        ((2, pieces, s.core, PIECE, d), BF16),
        ((2, pieces, PIECE, d), BF16),
        ((s.nx, s.nz, s.ny, PIECE, s.xw), BF16),
        ((s.nx - 1, s.nz, s.ny, PIECE, s.xw), BF16),
        ((s.nz, s.ny, PIECE, s.xw), BF16),
        ((s.nz - 1, s.ny, PIECE, s.xw), BF16),
        ((s.ny, PIECE, s.xw), BF16),
        ((s.ny - 1, PIECE, s.xw), BF16),
        ((s.nx, PIECE, s.xw), F32),
        ((s.ny, s.nz, PIECE, d), BF16),
        ((s.ny - 1, s.nz, PIECE, d), BF16),
        ((s.nz, PIECE, d), BF16),
        ((s.nz, PIECE, d), BF16),
        ((s.nx, PIECE, d), BF16),
    ]
    semaphores = [
        (9,),
        (recs, 2),
        (recs, 2),
        (),
        (2, s.group),
        (2, s.group),
        (2, s.nz),
        (2, s.nz),
        (2, 2, 2),
        (s.nx,),
        (s.nx,),
        (s.nz,),
        (s.nz,),
        (s.ny,),
        (s.ny,),
        (s.nx,),
        (s.nx,),
        (2, s.ny),
        (2, s.ny),
        (s.nz,),
        (s.nz,),
        (s.nx,),
        (s.nx,),
        (s.nz,),
        (s.nz,),
        (s.nx,),
        (s.nx,),
        (s.group,),
        (s.group,),
        (s.nz,),
        (s.nz,),
    ]
    gin, packed = pl.pallas_call(
        functools.partial(kernel, s),
        out_shape=(
            jax.ShapeDtypeStruct((recs, t, d), BF16),
            jax.ShapeDtypeStruct((48, d), F32),
        ),
        in_specs=[smem] + [hbm] * 9,
        out_specs=(hbm, vmem),
        scratch_shapes=[pltpu.VMEM(shape, dtype) for shape, dtype in buffers]
        + [dma if shape == () else dma(shape) for shape in semaphores],
        compiler_params=pltpu.CompilerParams(
            collective_id=0, has_side_effects=True, vmem_limit_bytes=56 * 1024 * 1024
        ),
        cost_estimate=pl.CostEstimate(
            flops=2 * 5 * recs * t * d * 2 * d, bytes_accessed=6 << 20, transcendentals=0
        ),
    )(
        dilation,
        retain,
        conv_w,
        skip_gain.reshape(1, d),
        log_rate.reshape(1, d),
        mode_angle.reshape(1, d),
        activations,
        cotangent,
        w_in,
        w_out,
    )
    grad_input, taps, skip, rate, angle, grad_w_in, grad_w_out = pl.pallas_call(
        spread,
        out_shape=(
            jax.ShapeDtypeStruct((recs, t, d), BF16),
            jax.ShapeDtypeStruct((TAPS, d), F32),
            jax.ShapeDtypeStruct((1, d), F32),
            jax.ShapeDtypeStruct((1, d), F32),
            jax.ShapeDtypeStruct((1, d), F32),
            jax.ShapeDtypeStruct((8, 2 * d), F32),
            jax.ShapeDtypeStruct((16, d), F32),
        ),
        in_specs=[vmem] * 2,
        out_specs=(vmem,) * 7,
    )(gin, packed)
    return (
        grad_input,
        taps,
        skip.reshape(d),
        rate.reshape(d),
        angle.reshape(d),
        grad_w_in,
        grad_w_out,
    )


def build(mesh, lag):
    wide = P("rec", "tm", None)
    return jax.shard_map(
        functools.partial(on_device, lag),
        mesh=mesh,
        in_specs=(wide, wide, P("rec", "tm")) + (P(),) * 7,
        out_specs=(wide, P(), P(), P(), P(), P("tm", None), P("tm", None)),
        check_vma=False,
    )


def solution(mesh):
    return build(mesh, MAXLAG)
```
